256 devices in a mesh: seq: 8 (over x, z_hi), cand: 32 (over z_lo, y, core).
Axes of the slice: x: 4, y: 4, z: 8 (z_hi: 2, z_lo: 4; z = z_hi * 4 + z_lo), core: 2. Of those that a mesh axis runs over, the one named last changes fastest.
Arguments:
- hist_x: bfloat16 [32, 1024, 1024], P('cand', 'seq'), may hold values from -6 to 6
- hist_len: int32 [32], replicated, may hold values from 1 to 1024, 20480 in all
- cand_x: bfloat16 [16384, 1024], P('cand'), may hold values from -6 to 6
- cand_user: int32 [16384, 1], P('cand'), may hold values from 0 to 31; in each aligned block of 512 rows (0 to 511, 512 to 1023, ...) at most 32 rows name the same one
- w_proj: bfloat16 [1024, 4096], replicated, may hold values from -0.1875 to 0.1875
- w_out: bfloat16 [1024, 1024], replicated, may hold values from -0.1875 to 0.1875
- norm_gain: float32 [1024], replicated, may hold values from 0.1 to 1.9
Outputs:
- hist_out: bfloat16 [32, 1024, 1024], P('cand', 'seq')
- cand_out: bfloat16 [16384, 1024], P('cand')
The draws below stay inside these ranges and needn't reach their ends.
Inputs may be any that keep to these rules, and one draw needn't show every extreme that they name: `cand_user`: of the 512 rows on one index of cand, at most 32 belong to one user. `hist_len`: the longest history has exactly 1024 events.
All inputs are finite; a program needn't handle non-finite values.
Results may differ from the reference program's by a relative error of at most 0.011.
Values may be sent and summed in bfloat16 or wider, within the bound.
A program may use at most 128 MiB of HBM per device.

```python
import math
import jax
import jax.numpy as jnp
import numpy as np
from jax import lax

D = 1024
HEADS = 8
HEAD = 128
C_DEV = 512
HIST = 1024
USERS = 32
CANDS = 16384
CAP = 32
N_CAND = 32


def block_levels(stream_key, dims, pieces, least, top_value):
    gain = 1.0
    for dim, blocks in pieces:
        heights = jax.random.uniform(jax.random.fold_in(jax.random.fold_in(stream_key, 6), dim), (blocks,), jnp.float32, least / len(pieces), top_value / len(pieces))
        gain = gain * jnp.repeat(jnp.exp(heights), dims[dim] // blocks).reshape((-1,) + (1,) * (len(dims) - 1 - dim))
    return gain


def length_profile(number_of, total, most, slope):
    weights = [(1 << 20) // math.isqrt(rank ** slope) + 1 for rank in range(2, number_of + 1)]
    spare, holding = total - most - (number_of - 1), [1] * (number_of - 1)
    while spare > 0:
        free = [i for i in range(number_of - 1) if holding[i] < most]
        pool, remaining = sum([weights[i] for i in free]), spare
        for i in free:
            more = min(most - holding[i], max(1, remaining * weights[i] // pool), spare)
            holding[i] = holding[i] + more
            spare = spare - more
    return np.array([most] + holding)


def uneven(key, number_of, total, reach, slope):
    if number_of == 2:
        one = jax.random.randint(key, (), max(1, total - reach), min(reach, total - 1) + 1)
        return jnp.stack([one, total - one])
    tallies = jnp.asarray(length_profile(number_of, total, reach, slope), jnp.int32)
    twos = (number_of - 1) // 2
    source_of, taker = tallies[1:1 + 2 * twos:2], tallies[2:2 + 2 * twos:2]
    margin = jnp.minimum(source_of - 1, reach - taker)
    passed = jax.random.randint(jax.random.fold_in(key, 1), (twos,), 0, 1 << 20) % (margin + 1)
    tallies = tallies.at[1:1 + 2 * twos:2].set(source_of - passed).at[2:2 + 2 * twos:2].set(taker + passed)
    return tallies[jax.random.permutation(jax.random.fold_in(key, 2), number_of)]


def routed_block(rng, own, number, rows, number_of, top, reach, slope):
    sequence = jax.random.permutation(rng, number_of)
    heavy_load, ordinary = portions_of(number_of, rows * top, reach, slope, True), portions_of(number_of, rows * top, reach, slope, False)
    places = jnp.arange(number_of)

    def named(tallies, rotation):
        used = int((tallies > 0).sum())
        fixed = max(1, used // 4)
        moved = fixed + (places - fixed + rotation * (used - fixed)) % max(1, number_of - fixed)
        return jnp.zeros((number_of,), jnp.int32).at[sequence[jnp.where(places < fixed, places, moved)]].set(jnp.asarray(tallies, jnp.int32))

    tallies = jnp.where(number % 4 == 0, named(heavy_load, number // 4), named(ordinary, number - number // 4 - 1))
    mixed = jax.random.permutation(jax.random.fold_in(own, 3), number_of)
    source_of, sink = mixed[0:number_of // 2 * 2:2], mixed[1:number_of // 2 * 2:2]
    slack = jnp.minimum(tallies[source_of] - 1, reach - tallies[sink]) // 2
    slack = jnp.where((source_of == sequence[0]) | (sink == sequence[0]) | (tallies[sink] == 0), 0, jnp.maximum(slack, 0))
    moved = jax.random.randint(jax.random.fold_in(own, 4), (number_of // 2,), 0, 1 << 20) % (slack + 1)
    tallies = tallies.at[source_of].add(-moved).at[sink].add(moved)
    items = jnp.searchsorted(jnp.cumsum(tallies), jnp.arange(rows * top), side="right").astype(jnp.int32)
    grid = items.reshape(top, rows).T
    grid = grid[jax.random.permutation(jax.random.fold_in(own, 1), rows)]
    rotation = jax.random.randint(jax.random.fold_in(own, 2), (rows, 1), 0, top)
    return jnp.take_along_axis(grid, (jnp.arange(top)[None, :] + rotation) % top, axis=1)


def portions_of(amount, total, limit, skew, full):
    weights = [(1 << 20) // math.isqrt(grade ** skew) + 1 for grade in range(1, amount + 1)]
    largest = limit if full else min(limit, max(-(-total // amount), total * weights[0] // sum(weights)))
    least = 1 if total - largest >= amount - 1 else 0
    given, rest = [largest] + [least] * (amount - 1), total - largest - least * (amount - 1)
    while rest > 0:
        free = [i for i in range(1, amount) if given[i] < largest] or [i for i in range(1, amount) if given[i] < limit]
        mass, left = sum([weights[i] for i in free]), rest
        for i in free:
            extra = min(limit - given[i], max(1, left * weights[i] // mass), rest)
            given[i] = given[i] + extra
            rest = rest - extra
    return np.array(given)


def normal_values(own_key, shape, spread, reach, shards=(), held_as=jnp.bfloat16):
    array = jax.random.normal(own_key, shape, jnp.float32) * spread
    if len(shards) > 0:
        array = block_levels(own_key, shape, shards, -0.22, 0.18) * array
    return jnp.clip(array, min=-reach, max=reach).astype(held_as)


def setup_inputs(seed: int = 0) -> dict:
    arg_keys = jax.random.split(jax.random.key(seed), 8)
    hist_x = normal_values(arg_keys[0], (USERS, HIST, D), 1.0, 6.0, ((0, 32), (1, 8)))
    hist_len = uneven(arg_keys[1], USERS, USERS * HIST * 5 // 8, HIST, 1).astype(jnp.int32)
    cand_x = normal_values(arg_keys[2], (CANDS, D), 1.0, 6.0, ((0, 32),))
    cand_user_keys = jax.random.split(jax.random.fold_in(arg_keys[3], 1), CANDS // C_DEV)
    cand_user_turns = jax.random.permutation(jax.random.fold_in(arg_keys[3], 3), CANDS // C_DEV)
    cand_user = jax.vmap(lambda own, number: routed_block(jax.random.fold_in(arg_keys[3], 2), own, number, C_DEV, USERS, 1, CAP, 2))(cand_user_keys, cand_user_turns).reshape((CANDS, 1))
    w_proj = normal_values(arg_keys[4], (D, 4 * D), D ** -0.5, 0.1875)
    w_out = normal_values(arg_keys[5], (D, D), D ** -0.5, 0.1875)
    norm_gain = jnp.clip(1.0 + 0.18 * jax.random.normal(arg_keys[6], (D,), jnp.float32), 0.1, 1.9)
    return dict(hist_x=hist_x, hist_len=hist_len, cand_x=cand_x, cand_user=cand_user, w_proj=w_proj, w_out=w_out, norm_gain=norm_gain)


def finish_rows(totals, norm_gain, gate_rows, inputs, w_out):
    average = lax.optimization_barrier(jnp.mean(totals, axis=-1, keepdims=True))
    centred = totals - average
    variance = lax.optimization_barrier(jnp.mean(centred * centred, axis=-1, keepdims=True))
    normed = (centred * lax.rsqrt(variance + 1e-05) * norm_gain * gate_rows.astype(jnp.float32)).astype(jnp.bfloat16)
    result = jnp.dot(normed, w_out, preferred_element_type=jnp.float32) + inputs.astype(jnp.float32)
    return result.astype(jnp.bfloat16)

def reference(hist_x, hist_len, cand_x, cand_user, w_proj, w_out, norm_gain):
    scale_qk = HEAD ** (-0.5)
    query_block = 512 if HIST % 512 == 0 else HIST
    block_count = HIST // query_block

    def encode(packed):
        history, length = packed
        projected = jax.nn.silu(jnp.dot(history, w_proj, preferred_element_type=jnp.float32)).astype(jnp.bfloat16)
        gate_hist = projected[:, :D]
        value_hist = projected[:, D:2 * D]
        query_hist = projected[:, 2 * D:3 * D]
        key_hist = projected[:, 3 * D:]
        key_heads = key_hist.astype(jnp.float32).reshape(HIST, HEADS, HEAD)
        value_heads = value_hist.astype(jnp.float32).reshape(HIST, HEADS, HEAD)
        key_position = jnp.arange(HIST, dtype=jnp.int32)
        query_blocks = query_hist.astype(jnp.float32).reshape(block_count, query_block, HEADS, HEAD)
        position_blocks = key_position.reshape(block_count, query_block)

        def one_block(items):
            query_heads, position = items
            scores = jnp.einsum('qhe,khe->hqk', query_heads, key_heads) * scale_qk
            allowed = (key_position[None, :] <= position[:, None]) & (key_position[None, :] < length)
            weights = jnp.where(allowed[None], jax.nn.silu(scores), 0.0).astype(jnp.bfloat16)
            weights = lax.optimization_barrier(weights).astype(jnp.float32)
            return jnp.einsum('hqk,khe->qhe', weights, value_heads).reshape(query_block, D)
        mixed_out = lax.map(one_block, (query_blocks, position_blocks)).reshape(HIST, D)
        return (finish_rows(mixed_out, norm_gain, gate_hist, history, w_out), key_hist, value_hist)
    hist_out, keys_all, values_all = lax.map(encode, (hist_x, hist_len))
    gate_cand = jax.nn.silu(jnp.dot(cand_x, w_proj[:, :D], preferred_element_type=jnp.float32)).astype(jnp.bfloat16)
    query_cand = jax.nn.silu(jnp.dot(cand_x, w_proj[:, 2 * D:3 * D], preferred_element_type=jnp.float32)).astype(jnp.bfloat16)
    owners = cand_user[:, 0].astype(jnp.int32)
    order = jnp.argsort(owners, stable=True).astype(jnp.int32)
    counts = lax.optimization_barrier(jnp.sum((owners[:, None] == jnp.arange(USERS, dtype=jnp.int32)[None, :]).astype(jnp.int32), axis=0)).astype(jnp.int32)
    starts = (jnp.cumsum(counts) - counts).astype(jnp.int32)
    most_rows = CAP * N_CAND
    padded_order = jnp.concatenate([order, jnp.zeros((most_rows,), jnp.int32)])

    def cross(user):
        picked = lax.dynamic_slice(padded_order, (starts[user].astype(jnp.int32),), (most_rows,))
        valid = jnp.arange(most_rows, dtype=jnp.int32) < counts[user]
        query_heads = query_cand[picked].astype(jnp.float32).reshape(most_rows, HEADS, HEAD)
        key_heads = keys_all[user].astype(jnp.float32).reshape(HIST, HEADS, HEAD)
        value_heads = values_all[user].astype(jnp.float32).reshape(HIST, HEADS, HEAD)
        scores = jnp.einsum('bhe,khe->hbk', query_heads, key_heads) * scale_qk
        allowed = jnp.arange(HIST, dtype=jnp.int32) < hist_len[user]
        weights = jnp.where(allowed[None, None, :], jax.nn.silu(scores), 0.0).astype(jnp.bfloat16)
        weights = lax.optimization_barrier(weights).astype(jnp.float32)
        mixed_rows = jnp.einsum('hbk,khe->bhe', weights, value_heads).reshape(most_rows, D)
        destination = jnp.where(valid, picked, CANDS).astype(jnp.int32)
        return (mixed_rows, destination)
    crossed_rows, destinations = lax.map(cross, jnp.arange(USERS, dtype=jnp.int32))
    crossed = jnp.zeros((CANDS + 1, D), jnp.float32).at[destinations.reshape(-1)].set(crossed_rows.reshape(-1, D))[:CANDS]
    cand_out = finish_rows(crossed, norm_gain, gate_cand, cand_x, w_out)
    return (hist_out, cand_out)
```

```python
import jax
import jax.numpy as jnp
from jax import lax
from jax.experimental import pallas as pl
from jax.experimental.pallas import tpu as pltpu
from jax.sharding import PartitionSpec as P


HEADS = 8
HEAD = 128
D = 1024
ROWS = 128
CHUNKS = 4
CROWS = ROWS // CHUNKS
CAND = 512
QUARTER = 256
MESH = pl.DeviceIdType.MESH
BF = jnp.bfloat16
F32 = jnp.float32
I32 = jnp.int32
NT = (((1,), (1,)), ((), ()))


def silu(a):
    half = 0.5 * a
    return half + half * jnp.tanh(half)


def iota(shape, dim):
    return lax.broadcasted_iota(I32, shape, dim)


def onehot(condition):
    return jnp.where(condition, 1.0, 0.0).astype(BF)


def dot(a, b):
    return jnp.dot(a, b, preferred_element_type=F32)


def remote(src, dst, send, recv, seq, cand):
    return pltpu.make_async_remote_copy(
        src_ref=src, dst_ref=dst, send_sem=send, recv_sem=recv,
        device_id={"seq": seq, "cand": cand}, device_id_type=MESH,
    )


def kernel(
    x_hbm, len_ref, candx_hbm, cuser_ref, wp_hbm, wo_hbm, gain_ref,
    hist_ref, cand_ref,
    wp, wo, candx, xb, keys, values, xq, qg, acc, msgs, rdisp, back, rret, crep, unsort, sorted_rows, hist_tmp,
    load_sem, swap_send, swap_recv, x_send, x_recv, fwd_send, d_send, d_recv, r_send, r_recv, g_send, g_recv, h_sem,
):
    s = lax.axis_index("seq")
    c = lax.axis_index("cand")
    x, zh = s // 2, s % 2
    core, y, zl = c % 2, (c // 2) % 4, c // 8
    z = zh * 4 + zl
    user = c - core + zh
    other_core = c + 1 - 2 * core
    early = core == zh
    late = core != zh
    swap_seq = 2 * x + core
    my_row = pl.multiple_of((core * 4 + x) * ROWS, ROWS)

    barrier = pltpu.get_barrier_semaphore()

    def greet(i, carry):
        pl.semaphore_signal(
            barrier, inc=1, device_id={"seq": 2 * x + (zh + i // 32) % 2, "cand": (c + i) % 32}, device_id_type=MESH
        )
        return carry

    lax.fori_loop(1, 64, greet, 0)
    for i in range(1, 4):
        pl.semaphore_signal(
            barrier, inc=1, device_id={"seq": 2 * ((x + i) % 4) + zh, "cand": c}, device_id_type=MESH
        )

    def load(src, dst, i):
        return pltpu.make_async_copy(src, dst, load_sem.at[i])

    own_load = load(x_hbm, xb.at[pl.ds(my_row, ROWS)], 0)
    cand_load = load(candx_hbm, candx, 1)
    wp_load = load(wp_hbm, wp, 2)
    wo_load = load(wo_hbm, wo, 3)

    @pl.when(early)
    def _():
        own_load.start()

    cand_load.start()
    wp_load.start()
    wo_load.start()

    @pl.when(early)
    def _():
        own_load.wait()

    pl.semaphore_wait(barrier, 66)

    def swap_copy(j):
        rows = pl.ds(pl.multiple_of((zh * 4 + x) * ROWS + j * CROWS, CROWS), CROWS)
        return remote(
            x_hbm.at[pl.ds(j * CROWS, CROWS)], xb.at[rows], swap_send.at[j], swap_recv.at[j], swap_seq, user
        )

    def own_rows(j):
        return xb.at[pl.ds(pl.multiple_of(my_row + j * CROWS, CROWS), CROWS)]

    def own_copy(i, j):
        recv = x_recv.at[(core * 4 + x) * CHUNKS + j]
        if i == 0:
            return remote(own_rows(j), own_rows(j), x_send.at[j], recv, s, other_core)
        return remote(own_rows(j), own_rows(j), x_send.at[i * CHUNKS + j], recv, 2 * ((x + i) % 4) + zh, c)

    def slot_rows(slot, j):
        return xb.at[pl.ds(pl.multiple_of(slot * ROWS + j * CROWS, CROWS), CROWS)]

    def slot_wait(slot, j):
        rows = slot_rows(slot, j)
        recv = x_recv.at[slot * CHUNKS + j]
        remote(rows, rows, fwd_send.at[0], recv, s, other_core).wait_recv()

    def fwd_copy(i, j):
        slot = core * 4 + (x + i) % 4
        rows = slot_rows(slot, j)
        return remote(rows, rows, fwd_send.at[(i - 1) * CHUNKS + j], x_recv.at[slot * CHUNKS + j], s, other_core)

    def forward():
        for j in range(CHUNKS):
            for i in range(1, 4):
                slot_wait(core * 4 + (x + i) % 4, j)
                fwd_copy(i, j).start()

    @pl.when(late)
    def _():
        for j in range(CHUNKS):
            swap_copy(j).start()

    @pl.when(early)
    def _():
        for j in range(CHUNKS):
            for i in range(4):
                own_copy(i, j).start()

    owner = cuser_ref[...]
    is_user = owner == iota((32, CAND), 0)
    users = onehot(is_user)
    before = dot(users, onehot(iota((CAND, CAND), 0) < iota((CAND, CAND), 1)))
    within = jnp.sum(jnp.where(is_user, before, 0.0), axis=0, keepdims=True).astype(I32)
    smaller = dot(onehot(iota((32, 32), 1) < iota((32, 32), 0)), users)
    start = jnp.sum(smaller, axis=1, keepdims=True)
    place = jnp.sum(jnp.where(is_user, start, 0.0), axis=0, keepdims=True).astype(I32) + within
    part = place & 7
    code = owner * 32 + part * 4 + (within >> 3)
    sorted_at = ((part >> 1) << 7) + ((part & 1) << 6) + (place >> 3)

    def message(m):
        which, dy = m >> 2, m & 3
        pair = which >> 1
        dz = jnp.where(
            pair == 0, 0, jnp.where(pair == 1, 1, jnp.where(pair == 2, 7, jnp.where(which == 6, 2, 6)))
        )
        dcore = which & 1
        tz = (z + dz) & 7
        ty = (y + dy) & 3
        tcore = (core + dcore) & 1
        column = (tz & 3) * 4 + ty
        return column * 2 + (tz >> 2), tz >> 2, column * 2 + tcore, tcore

    slot = iota((CAND, 1), 0)
    to_user, _, _, to_core = message(slot >> 4)
    slot_code = to_user * 32 + (2 * x + to_core) * 4 + (slot & 3)
    match = slot_code == code
    slot_quarter = (slot >> 2) & 3
    cand_load.wait()
    sent = jnp.zeros((CAND, QUARTER), F32)
    for j in range(4):
        sent += dot(onehot(match & (slot_quarter == j)), candx[:, j * QUARTER : (j + 1) * QUARTER])
    msgs[...] = sent.astype(BF)

    def piece(ref, i):
        return ref.at[pl.ds(pl.multiple_of(i * 16, 16), 16)]

    def d_copy(m):
        _, tzh, tcand, _ = message(m)
        return remote(piece(msgs, m), piece(rdisp, c), d_send.at[m], d_recv.at[c], 2 * x + tzh, tcand)

    self_d = pltpu.make_async_copy(piece(msgs, 0), piece(rdisp, c), d_recv.at[c])
    self_d.start()

    def send_d(m, carry):
        d_copy(m).start()
        return carry

    lax.fori_loop(1, 32, send_d, 0)

    ret = iota((1024, 1), 0)
    ret_to = ret >> 4
    ret_code = (ret_to >> 1) * 32 + (2 * x + (ret_to & 1)) * 4 + (ret & 3)
    mine = iota((ROWS, 1), 0)
    mine_place = 8 * (mine & 63) + 2 * x + (mine >> 6)
    crep[...] = lax.dot_general(
        onehot(mine_place == place), onehot(ret_code == code), NT, preferred_element_type=F32
    ).astype(BF)
    unsort[...] = lax.dot_general(
        onehot(iota((CAND, CAND), 0) == iota((CAND, CAND), 1)),
        onehot(iota((CAND, 1), 0) == sorted_at), NT, preferred_element_type=F32,
    ).astype(BF)

    @pl.when(late)
    def _():
        for j in range(CHUNKS):
            swap_copy(j).wait_recv()
            for i in range(4):
                own_copy(i, j).start()

    @pl.when(early)
    def _():
        forward()

    length = len_ref[user]

    def block_pos(kind, width_iota):
        return (2 * (width_iota >> 7) + kind) * ROWS + (width_iota & (ROWS - 1))

    def project(kind):
        top = pl.multiple_of(kind * 4 * ROWS, ROWS)
        rows = pl.ds(top, 4 * ROWS)
        alive = block_pos(kind, iota((4 * ROWS, 1), 0)) < length

        def step(n, carry):
            cols = pl.ds(pl.multiple_of(n * QUARTER, QUARTER), QUARTER)
            kcols = pl.ds(pl.multiple_of(3 * D + n * QUARTER, QUARTER), QUARTER)
            vcols = pl.ds(pl.multiple_of(D + n * QUARTER, QUARTER), QUARTER)
            keys[rows, cols] = silu(dot(xb[rows, :], wp[:, kcols])).astype(BF)
            values[rows, cols] = jnp.where(alive, silu(dot(xb[rows, :], wp[:, vcols])), 0.0).astype(BF)
            return carry

        lax.fori_loop(0, 4, step, 0)

    query_row = iota((2 * ROWS, 1), 0)
    query_pos = jnp.where(query_row < ROWS, (2 * x + core) * ROWS + query_row, 1 << 20)

    def attend(kind, first):
        top = pl.multiple_of(kind * 4 * ROWS, ROWS)
        rows = pl.ds(top, 4 * ROWS)
        allowed = block_pos(kind, iota((1, 4 * ROWS), 1)) <= query_pos

        def step(h, carry):
            cols = pl.ds(pl.multiple_of(h * HEAD, HEAD), HEAD)
            scores = lax.dot_general(qg[:, pl.ds(pl.multiple_of(D + h * HEAD, HEAD), HEAD)], keys[rows, cols], NT,
                                     preferred_element_type=F32)
            weights = jnp.where(allowed, silu(scores * HEAD ** -0.5), 0.0).astype(BF)
            mixed = dot(weights, values[rows, cols])
            if first:
                acc[:, cols] = mixed
            else:
                acc[:, cols] += mixed
            return carry

        lax.fori_loop(0, HEADS, step, 0)

    wp_load.wait()

    @pl.when(late)
    def _():
        for j in range(CHUNKS):
            for i in range(4):
                slot_wait((1 - core) * 4 + (x + i) % 4, j)

    project(zh)

    def wait_d(i, carry):
        there = (c + i) % 32
        remote(piece(rdisp, there), piece(rdisp, there), d_send.at[0], d_recv.at[there], s, other_core).wait_recv()
        return carry

    self_d.wait()
    lax.fori_loop(1, 32, wait_d, 0)
    here = iota((ROWS, CAND), 0)
    lane = iota((ROWS, CAND), 1)
    same = ((here >> 2) == (lane >> 4)) & ((here & 3) == (lane & 3))
    lane_quarter = (lane >> 2) & 3
    for j in range(4):
        xq[ROWS : 2 * ROWS, j * QUARTER : (j + 1) * QUARTER] = dot(
            onehot(same & (lane_quarter == j)), rdisp[...]
        ).astype(BF)
    xq[0:ROWS, :] = xb[pl.ds(my_row, ROWS), :]

    def project_q(n, carry):
        cols = pl.ds(pl.multiple_of(n * QUARTER, QUARTER), QUARTER)
        qcols = pl.ds(pl.multiple_of(D + n * QUARTER, QUARTER), QUARTER)
        wcols = pl.ds(pl.multiple_of(2 * D + n * QUARTER, QUARTER), QUARTER)
        qg[:, cols] = silu(dot(xq[...], wp[:, cols])).astype(BF)
        qg[:, qcols] = silu(dot(xq[...], wp[:, wcols])).astype(BF)
        return carry

    lax.fori_loop(0, 4, project_q, 0)
    attend(zh, True)

    @pl.when(late)
    def _():
        forward()

    @pl.when(early)
    def _():
        for j in range(CHUNKS):
            for i in range(4):
                slot_wait((1 - core) * 4 + (x + i) % 4, j)

    project(1 - zh)
    attend(1 - zh, False)

    wo_load.wait()

    def finish(first):
        rows = slice(first, first + ROWS)
        totals = acc[rows, :]
        average = jnp.mean(totals, axis=1, keepdims=True)
        centred = totals - average
        variance = jnp.mean(centred * centred, axis=1, keepdims=True)
        normed = (
            centred * lax.rsqrt(variance + 1e-05) * gain_ref[...] * qg[rows, 0:D].astype(F32)
        ).astype(BF)
        return (dot(normed, wo[...]) + xq[rows, :].astype(F32)).astype(BF)

    done = finish(ROWS)
    tall = iota((CAND, ROWS), 0)
    wide = iota((CAND, ROWS), 1)
    same_t = ((wide >> 2) == (tall >> 4)) & ((wide & 3) == (tall & 3))
    tall_quarter = (tall >> 2) & 3
    returned = jnp.zeros((CAND, QUARTER), F32)
    for j in range(4):
        returned += dot(onehot(same_t & (tall_quarter == j)), done[:, j * QUARTER : (j + 1) * QUARTER])
    back[...] = returned.astype(BF)
    my_ret = user * 2 + core

    def r_copy(i):
        there = (c + i) % 32
        return remote(
            piece(back, there), piece(rret, my_ret), r_send.at[i], r_recv.at[my_ret], 2 * x + (zh + i // 32) % 2, there
        )

    self_r = pltpu.make_async_copy(piece(back, c), piece(rret, my_ret), r_recv.at[my_ret])
    self_r.start()

    def send_r(i, carry):
        r_copy(i).start()
        return carry

    lax.fori_loop(1, 64, send_r, 0)

    done_hist = finish(0)
    hist_copy = remote(hist_tmp, hist_ref, h_sem.at[0], h_sem.at[1], swap_seq, user)

    @pl.when(early)
    def _():
        hist_ref[...] = done_hist

    @pl.when(late)
    def _():
        hist_tmp[...] = done_hist
        hist_copy.start()

    def wait_r(i, carry):
        there = (my_ret + i) % 64
        remote(piece(rret, there), piece(rret, there), d_send.at[0], r_recv.at[there], s, other_core).wait_recv()
        return carry

    self_r.wait()
    lax.fori_loop(1, 64, wait_r, 0)
    mine_rows = pl.ds(pl.multiple_of(x * ROWS, ROWS), ROWS)
    ret_quarter = (iota((ROWS, 1024), 1) >> 2) & 3
    for j in range(4):
        picked = jnp.where(ret_quarter == j, crep[...], jnp.zeros((), BF))
        sorted_rows[mine_rows, j * QUARTER : (j + 1) * QUARTER] = dot(picked, rret[...]).astype(BF)

    def g_copy(i):
        return remote(
            sorted_rows.at[mine_rows], sorted_rows.at[mine_rows], g_send.at[i], g_recv.at[x], 2 * ((x + i) % 4) + zh, c
        )

    for i in range(1, 4):
        g_copy(i).start()
    for i in range(1, 4):
        from_x = (x + i) % 4
        rows = sorted_rows.at[pl.ds(pl.multiple_of(from_x * ROWS, ROWS), ROWS)]
        remote(rows, rows, g_send.at[0], g_recv.at[from_x], s, other_core).wait_recv()

    def last(n, carry):
        cols = pl.ds(pl.multiple_of(n * QUARTER, QUARTER), QUARTER)
        cand_ref[:, cols] = dot(unsort[...], sorted_rows[:, cols]).astype(BF)
        return carry

    lax.fori_loop(0, 4, last, 0)

    for i in range(1, 4):
        g_copy(i).wait_send()

    def sent_r(i, carry):
        r_copy(i).wait_send()
        return carry

    lax.fori_loop(1, 64, sent_r, 0)

    def sent_d(m, carry):
        d_copy(m).wait_send()
        return carry

    lax.fori_loop(1, 32, sent_d, 0)
    for j in range(CHUNKS):
        for i in range(4):
            own_copy(i, j).wait_send()
        for i in range(1, 4):
            fwd_copy(i, j).wait_send()

    @pl.when(late)
    def _():
        for j in range(CHUNKS):
            swap_copy(j).wait_send()
        hist_copy.wait()


def per_device(hist_x, hist_len, cand_x, cand_user, w_proj, w_out, norm_gain):
    any_spec = pl.BlockSpec(memory_space=pl.ANY)
    vmem = pl.BlockSpec(memory_space=pltpu.VMEM)
    dma = pltpu.SemaphoreType.DMA
    hist_out, cand_out = pl.pallas_call(
        kernel,
        out_shape=(jax.ShapeDtypeStruct((ROWS, D), BF), jax.ShapeDtypeStruct((CAND, D), BF)),
        in_specs=[any_spec, pl.BlockSpec(memory_space=pltpu.SMEM), any_spec, vmem, any_spec, any_spec, vmem],
        out_specs=(vmem, vmem),
        scratch_shapes=[
            pltpu.VMEM((D, 4 * D), BF),
            pltpu.VMEM((D, D), BF),
            pltpu.VMEM((CAND, D), BF),
            pltpu.VMEM((8 * ROWS, D), BF),
            pltpu.VMEM((8 * ROWS, D), BF),
            pltpu.VMEM((8 * ROWS, D), BF),
            pltpu.VMEM((2 * ROWS, D), BF),
            pltpu.VMEM((2 * ROWS, 2 * D), BF),
            pltpu.VMEM((2 * ROWS, D), F32),
            pltpu.VMEM((CAND, QUARTER), BF),
            pltpu.VMEM((CAND, QUARTER), BF),
            pltpu.VMEM((CAND, QUARTER), BF),
            pltpu.VMEM((2 * CAND, QUARTER), BF),
            pltpu.VMEM((ROWS, 2 * CAND), BF),
            pltpu.VMEM((CAND, CAND), BF),
            pltpu.VMEM((CAND, D), BF),
            pltpu.VMEM((ROWS, D), BF),
            dma((4,)),
            dma((CHUNKS,)),
            dma((CHUNKS,)),
            dma((4 * CHUNKS,)),
            dma((8 * CHUNKS,)),
            dma((3 * CHUNKS,)),
            dma((32,)),
            dma((32,)),
            dma((64,)),
            dma((64,)),
            dma((4,)),
            dma((4,)),
            dma((2,)),
        ],
        compiler_params=pltpu.CompilerParams(
            collective_id=0, has_side_effects=True, vmem_limit_bytes=56 * 2**20
        ),
    )(
        hist_x.reshape(ROWS, D), hist_len, cand_x, cand_user.reshape(1, CAND), w_proj, w_out,
        norm_gain.reshape(1, D),
    )
    return hist_out[None], cand_out


def solution(mesh):
    in_specs = (P("cand", "seq", None), P(), P("cand", None), P("cand", None), P(), P(), P())
    out_specs = (P("cand", "seq", None), P("cand", None))
    return jax.shard_map(
        per_device, mesh=mesh, in_specs=in_specs, out_specs=out_specs, check_vma=False
    )
```

```python
import jax
import jax.numpy as jnp
from jax import lax
from jax.experimental import pallas as pl
from jax.experimental.pallas import tpu as pltpu
from jax.sharding import PartitionSpec as P


HEADS = 8
HEAD = 128
D = 1024
ROWS = 128
CHUNKS = 4
CROWS = ROWS // CHUNKS
CAND = 512
QUARTER = 256
PARTS = 2
WIDE = D // PARTS
PIECE = WIDE // 4
MESH = pl.DeviceIdType.MESH
BF = jnp.bfloat16
F32 = jnp.float32
I32 = jnp.int32
NT = (((1,), (1,)), ((), ()))


def silu(a):
    half = 0.5 * a
    return half + half * jnp.tanh(half)


def iota(shape, dim):
    return lax.broadcasted_iota(I32, shape, dim)


def onehot(condition):
    return jnp.where(condition, 1.0, 0.0).astype(BF)


def dot(a, b):
    return jnp.dot(a, b, preferred_element_type=F32)


def remote(src, dst, send, recv, seq, cand):
    return pltpu.make_async_remote_copy(
        src_ref=src, dst_ref=dst, send_sem=send, recv_sem=recv,
        device_id={"seq": seq, "cand": cand}, device_id_type=MESH,
    )


def kernel(
    x_hbm, len_ref, candx_hbm, cuser_ref, wp_hbm, wo_hbm, gain_ref,
    hist_ref, sorted_rows, unsort,
    wp, wo, candx, xb, keys, values, xc, xh, qg, acc, normed_ref, msgs, rdisp, back, rret, crep, hist_tmp,
    load_sem, swap_send, swap_recv, x_send, x_recv, fwd_send, d_send, d_recv, r_send, r_recv, g_send, g_recv, h_sem,
):
    s = lax.axis_index("seq")
    c = lax.axis_index("cand")
    x, zh = s // 2, s % 2
    core, y, zl = c % 2, (c // 2) % 4, c // 8
    z = zh * 4 + zl
    user = c - core + zh
    other_core = c + 1 - 2 * core
    early = core == zh
    late = core != zh
    swap_seq = 2 * x + core

    barrier = pltpu.get_barrier_semaphore()

    def greet(i, carry):
        pl.semaphore_signal(
            barrier, inc=1, device_id={"seq": 2 * x + (zh + i // 32) % 2, "cand": (c + i) % 32}, device_id_type=MESH
        )
        return carry

    lax.fori_loop(1, 64, greet, 0)
    for i in range(1, 4):
        pl.semaphore_signal(
            barrier, inc=1, device_id={"seq": 2 * ((x + i) % 4) + zh, "cand": c}, device_id_type=MESH
        )

    def load(src, dst, i):
        return pltpu.make_async_copy(src, dst, load_sem.at[i])

    def slot_rows(kind, there, j):
        return xb.at[pl.ds(pl.multiple_of(kind * 4 * ROWS + j * ROWS + there * CROWS, CROWS), CROWS)]

    def own_load(j):
        return load(x_hbm.at[pl.ds(j * CROWS, CROWS)], slot_rows(core, x, j), 3 + j)

    cand_load = load(candx_hbm, candx, 0)
    wp_load = load(wp_hbm, wp, 1)
    wo_load = load(wo_hbm, wo, 2)

    @pl.when(early)
    def _():
        for j in range(CHUNKS):
            own_load(j).start()

    cand_load.start()
    wp_load.start()
    wo_load.start()

    @pl.when(early)
    def _():
        for j in range(CHUNKS):
            own_load(j).wait()

    pl.semaphore_wait(barrier, 66)

    def swap_copy(j):
        return remote(
            x_hbm.at[pl.ds(j * CROWS, CROWS)], slot_rows(zh, x, j), swap_send.at[j], swap_recv.at[j], swap_seq, user
        )

    def own_copy(i, j):
        rows = slot_rows(core, x, j)
        recv = x_recv.at[(core * 4 + x) * CHUNKS + j]
        if i == 0:
            return remote(rows, rows, x_send.at[j], recv, s, other_core)
        return remote(rows, rows, x_send.at[i * CHUNKS + j], recv, 2 * ((x + i) % 4) + zh, c)

    def slot_wait(kind, there, j):
        rows = slot_rows(kind, there, j)
        recv = x_recv.at[(kind * 4 + there) * CHUNKS + j]
        remote(rows, rows, fwd_send.at[0], recv, s, other_core).wait_recv()

    def fwd_copy(i, j):
        there = (x + i) % 4
        rows = slot_rows(core, there, j)
        recv = x_recv.at[(core * 4 + there) * CHUNKS + j]
        return remote(rows, rows, fwd_send.at[(i - 1) * CHUNKS + j], recv, s, other_core)

    def send_own(j):
        for i in range(4):
            own_copy(i, j).start()

    def forward(j):
        for i in range(1, 4):
            slot_wait(core, (x + i) % 4, j)
            fwd_copy(i, j).start()

    def take(j):
        for i in range(4):
            slot_wait(1 - core, (x + i) % 4, j)

    @pl.when(late)
    def _():
        for j in range(CHUNKS):
            swap_copy(j).start()

    @pl.when(early)
    def _():
        for j in range(CHUNKS):
            send_own(j)

    owner = cuser_ref[...]
    is_user = owner == iota((32, CAND), 0)
    users = onehot(is_user)
    before = dot(users, onehot(iota((CAND, CAND), 0) < iota((CAND, CAND), 1)))
    within = jnp.sum(jnp.where(is_user, before, 0.0), axis=0, keepdims=True).astype(I32)
    smaller = dot(onehot(iota((32, 32), 1) < iota((32, 32), 0)), users)
    start = jnp.sum(smaller, axis=1, keepdims=True)
    place = jnp.sum(jnp.where(is_user, start, 0.0), axis=0, keepdims=True).astype(I32) + within
    part = place & 7
    code = owner * 32 + part * 4 + (within >> 3)
    sorted_at = ((part >> 1) << 7) + ((part & 1) << 6) + (place >> 3)

    def message(m):
        which, dy = m >> 2, m & 3
        pair = which >> 1
        dz = jnp.where(
            pair == 0, 0, jnp.where(pair == 1, 1, jnp.where(pair == 2, 7, jnp.where(which == 6, 2, 6)))
        )
        dcore = which & 1
        tz = (z + dz) & 7
        ty = (y + dy) & 3
        tcore = (core + dcore) & 1
        column = (tz & 3) * 4 + ty
        return column * 2 + (tz >> 2), tz >> 2, column * 2 + tcore, tcore

    slot = iota((CAND, 1), 0)
    to_user, _, _, to_core = message(slot >> 4)
    slot_code = to_user * 32 + (2 * x + to_core) * 4 + (slot & 3)
    match = slot_code == code
    slot_quarter = (slot >> 2) & 3
    cand_load.wait()
    sent = jnp.zeros((CAND, QUARTER), F32)
    for j in range(4):
        sent += dot(onehot(match & (slot_quarter == j)), candx[:, j * QUARTER : (j + 1) * QUARTER])
    msgs[...] = sent.astype(BF)

    def piece(ref, i):
        return ref.at[pl.ds(pl.multiple_of(i * 16, 16), 16)]

    def d_copy(m):
        _, tzh, tcand, _ = message(m)
        return remote(piece(msgs, m), piece(rdisp, c), d_send.at[m], d_recv.at[c], 2 * x + tzh, tcand)

    self_d = pltpu.make_async_copy(piece(msgs, 0), piece(rdisp, c), d_recv.at[c])
    self_d.start()

    def send_d(m, carry):
        d_copy(m).start()
        return carry

    lax.fori_loop(1, 32, send_d, 0)

    ret = iota((1024, 1), 0)
    ret_to = ret >> 4
    ret_code = (ret_to >> 1) * 32 + (2 * x + (ret_to & 1)) * 4 + (ret & 3)
    mine = iota((ROWS, 1), 0)
    mine_place = 8 * (mine & 63) + 2 * x + (mine >> 6)
    places = lax.dot_general(
        onehot(mine_place == place), onehot(ret_code == code), NT, preferred_element_type=F32
    )
    ret_quarter = (iota((ROWS, 1024), 1) >> 2) & 3
    for j in range(4):
        crep[j * ROWS : (j + 1) * ROWS, :] = jnp.where(ret_quarter == j, places, 0.0).astype(BF)
    unsort[...] = lax.dot_general(
        onehot(iota((CAND, CAND), 0) == iota((CAND, CAND), 1)),
        onehot(iota((CAND, 1), 0) == sorted_at), NT, preferred_element_type=F32,
    ).astype(BF)

    length = len_ref[user]

    def block_pos(kind, row):
        return (2 * ((row >> 5) & 3) + kind) * ROWS + (row >> 7) * CROWS + (row & (CROWS - 1))

    def project(kind, pair):
        rows = pl.ds(pl.multiple_of((kind * 2 + pair) * 2 * ROWS, 2 * ROWS), 2 * ROWS)
        alive = block_pos(kind, pair * 2 * ROWS + iota((2 * ROWS, 1), 0)) < length

        def step(n, carry):
            cols = pl.ds(pl.multiple_of(n * QUARTER, QUARTER), QUARTER)
            kcols = pl.ds(pl.multiple_of(3 * D + n * QUARTER, QUARTER), QUARTER)
            vcols = pl.ds(pl.multiple_of(D + n * QUARTER, QUARTER), QUARTER)
            keys[rows, cols] = silu(dot(xb[rows, :], wp[:, kcols])).astype(BF)
            values[rows, cols] = jnp.where(alive, silu(dot(xb[rows, :], wp[:, vcols])), 0.0).astype(BF)
            return carry

        lax.fori_loop(0, 4, step, 0, unroll=2)

    def project_q(rows_ref):
        def step(n, carry):
            cols = pl.ds(pl.multiple_of(n * QUARTER, QUARTER), QUARTER)
            qcols = pl.ds(pl.multiple_of(D + n * QUARTER, QUARTER), QUARTER)
            wcols = pl.ds(pl.multiple_of(2 * D + n * QUARTER, QUARTER), QUARTER)
            qg[:, qcols] = silu(dot(rows_ref[...], wp[:, wcols])).astype(BF)
            qg[:, cols] = silu(dot(rows_ref[...], wp[:, cols])).astype(BF)
            return carry

        lax.fori_loop(0, 4, step, 0, unroll=2)

    def attend(top, count, allowed, first):
        rows = pl.ds(top, count)
        for h in range(HEADS):
            cols = slice(h * HEAD, (h + 1) * HEAD)
            scores = lax.dot_general(
                qg[:, D + h * HEAD : D + (h + 1) * HEAD], keys[rows, cols], NT, preferred_element_type=F32
            )
            weights = silu(scores * HEAD ** -0.5)
            if allowed is not None:
                weights = jnp.where(allowed, weights, 0.0)
            mixed = dot(weights.astype(BF), values[rows, cols])
            if first:
                acc[:, cols] = mixed
            else:
                acc[:, cols] += mixed

    def kind_top(kind):
        return pl.multiple_of(kind * 4 * ROWS, 4 * ROWS)

    wp_load.wait()
    for pair in range(2):
        for j in (2 * pair, 2 * pair + 1):
            @pl.when(late)
            def _():
                swap_copy(j).wait_recv()
                send_own(j)
                take(j)

            @pl.when(early)
            def _():
                forward(j)

        project(zh, pair)

    def late_forward(j):
        @pl.when(late)
        def _():
            forward(j)

    def early_take(j):
        @pl.when(early)
        def _():
            take(j)

    late_forward(0)

    def wait_d(i, carry):
        there = (c + i) % 32
        remote(piece(rdisp, there), piece(rdisp, there), d_send.at[0], d_recv.at[there], s, other_core).wait_recv()
        return carry

    self_d.wait()
    lax.fori_loop(1, 32, wait_d, 0)
    here = iota((ROWS, CAND), 0)
    lane = iota((ROWS, CAND), 1)
    same = ((here >> 2) == (lane >> 4)) & ((here & 3) == (lane & 3))
    lane_quarter = (lane >> 2) & 3
    for j in range(4):
        xc[:, j * QUARTER : (j + 1) * QUARTER] = dot(onehot(same & (lane_quarter == j)), rdisp[...]).astype(BF)
    project_q(xc)
    late_forward(1)
    attend(kind_top(zh), 4 * ROWS, None, True)
    late_forward(2)
    early_take(0)
    early_take(1)
    project(1 - zh, 0)
    late_forward(3)
    early_take(2)
    early_take(3)
    project(1 - zh, 1)
    attend(kind_top(1 - zh), 4 * ROWS, None, False)
    wo_load.wait()

    def normalise():
        totals = acc[...]
        average = jnp.mean(totals, axis=1, keepdims=True)
        centred = totals - average
        variance = jnp.mean(centred * centred, axis=1, keepdims=True)
        normed_ref[...] = (
            centred * lax.rsqrt(variance + 1e-05) * gain_ref[...] * qg[:, 0:D].astype(F32)
        ).astype(BF)

    def finish(rows_ref, cols):
        return (dot(normed_ref[...], wo[:, cols]) + rows_ref[:, cols].astype(F32)).astype(BF)

    normalise()
    tall = iota((CAND, ROWS), 0)
    wide = iota((CAND, ROWS), 1)
    same_t = ((wide >> 2) == (tall >> 4)) & ((wide & 3) == (tall & 3))
    tall_quarter = (tall >> 2) & 3
    my_ret = user * 2 + core

    def r_copy(i, part):
        there = (c + i) % 32
        return remote(
            piece(back, part * 32 + there), piece(rret, part * 64 + my_ret), r_send.at[part * 64 + i],
            r_recv.at[part * 64 + my_ret], 2 * x + (zh + i // 32) % 2, there,
        )

    def self_r(part):
        here_r = part * 64 + my_ret
        return pltpu.make_async_copy(piece(back, part * 32 + c), piece(rret, here_r), r_recv.at[here_r])

    for part in range(PARTS):
        done = finish(xc, slice(part * WIDE, (part + 1) * WIDE))
        returned = jnp.zeros((CAND, PIECE), F32)
        for j in range(4):
            returned += dot(onehot(same_t & (tall_quarter == j)), done[:, j * PIECE : (j + 1) * PIECE])
        back[part * CAND : (part + 1) * CAND, :] = returned.astype(BF)
        self_r(part).start()

        def send_r(i, carry):
            r_copy(i, part).start()
            return carry

        lax.fori_loop(1, 64, send_r, 0)

    for j in range(CHUNKS):
        xh[j * CROWS : (j + 1) * CROWS, :] = slot_rows(core, x, j)[...]
    project_q(xh)
    query_pos = (2 * x + core) * ROWS + iota((ROWS, 1), 0)
    key = iota((1, 8 * ROWS), 1)
    attend(0, 8 * ROWS, block_pos(key >> 9, key & 511) <= query_pos, True)
    normalise()
    done_hist = finish(xh, slice(0, D))
    hist_copy = remote(hist_tmp, hist_ref, h_sem.at[0], h_sem.at[1], swap_seq, user)

    @pl.when(early)
    def _():
        hist_ref[...] = done_hist

    @pl.when(late)
    def _():
        hist_tmp[...] = done_hist

    def sorted_part(part, there):
        return sorted_rows.at[pl.ds(pl.multiple_of(part * CAND + there * ROWS, ROWS), ROWS)]

    def g_copy(i, part):
        rows = sorted_part(part, x)
        return remote(
            rows, rows, g_send.at[part * 4 + i], g_recv.at[part * 4 + x], 2 * ((x + i) % 4) + zh, c
        )

    for part in range(PARTS):
        self_r(part).wait()

        def wait_r(i, carry):
            there = part * 64 + (my_ret + i) % 64
            remote(piece(rret, there), piece(rret, there), d_send.at[0], r_recv.at[there], s, other_core).wait_recv()
            return carry

        lax.fori_loop(1, 64, wait_r, 0)
        picked = dot(crep[...], rret[part * 1024 : (part + 1) * 1024, :]).astype(BF)
        rows = pl.ds(pl.multiple_of(part * CAND + x * ROWS, ROWS), ROWS)
        for j in range(4):
            sorted_rows[rows, j * PIECE : (j + 1) * PIECE] = picked[j * ROWS : (j + 1) * ROWS, :]
        for i in range(1, 4):
            g_copy(i, part).start()

    @pl.when(late)
    def _():
        hist_copy.start()

    for part in range(PARTS):
        for i in range(1, 4):
            from_x = (x + i) % 4
            rows = sorted_part(part, from_x)
            remote(rows, rows, g_send.at[0], g_recv.at[part * 4 + from_x], s, other_core).wait_recv()

    for part in range(PARTS):
        for i in range(1, 4):
            g_copy(i, part).wait_send()

        def sent_r(i, carry):
            r_copy(i, part).wait_send()
            return carry

        lax.fori_loop(1, 64, sent_r, 0)

    def sent_d(m, carry):
        d_copy(m).wait_send()
        return carry

    lax.fori_loop(1, 32, sent_d, 0)
    for j in range(CHUNKS):
        for i in range(4):
            own_copy(i, j).wait_send()
        for i in range(1, 4):
            fwd_copy(i, j).wait_send()

    @pl.when(late)
    def _():
        for j in range(CHUNKS):
            swap_copy(j).wait_send()
        hist_copy.wait()


def last_kernel(unsort, rows_ref, hist_in, hist_ref, cand_ref):
    cand_ref[...] = dot(unsort[...], rows_ref[...]).astype(BF)
    hist_ref[...] = hist_in[...]


def per_device(hist_x, hist_len, cand_x, cand_user, w_proj, w_out, norm_gain):
    any_spec = pl.BlockSpec(memory_space=pl.ANY)
    vmem = pl.BlockSpec(memory_space=pltpu.VMEM)
    dma = pltpu.SemaphoreType.DMA
    hist_rows, sorted_rows, unsort = pl.pallas_call(
        kernel,
        out_shape=(
            jax.ShapeDtypeStruct((ROWS, D), BF),
            jax.ShapeDtypeStruct((PARTS * CAND, WIDE), BF),
            jax.ShapeDtypeStruct((CAND, CAND), BF),
        ),
        in_specs=[any_spec, pl.BlockSpec(memory_space=pltpu.SMEM), any_spec, vmem, any_spec, any_spec, vmem],
        out_specs=(vmem, vmem, vmem),
        scratch_shapes=[
            pltpu.VMEM((D, 4 * D), BF),
            pltpu.VMEM((D, D), BF),
            pltpu.VMEM((CAND, D), BF),
            pltpu.VMEM((8 * ROWS, D), BF),
            pltpu.VMEM((8 * ROWS, D), BF),
            pltpu.VMEM((8 * ROWS, D), BF),
            pltpu.VMEM((ROWS, D), BF),
            pltpu.VMEM((ROWS, D), BF),
            pltpu.VMEM((ROWS, 2 * D), BF),
            pltpu.VMEM((ROWS, D), F32),
            pltpu.VMEM((ROWS, D), BF),
            pltpu.VMEM((CAND, QUARTER), BF),
            pltpu.VMEM((CAND, QUARTER), BF),
            pltpu.VMEM((PARTS * CAND, PIECE), BF),
            pltpu.VMEM((2 * PARTS * CAND, PIECE), BF),
            pltpu.VMEM((4 * ROWS, 2 * CAND), BF),
            pltpu.VMEM((ROWS, D), BF),
            dma((3 + CHUNKS,)),
            dma((CHUNKS,)),
            dma((CHUNKS,)),
            dma((4 * CHUNKS,)),
            dma((8 * CHUNKS,)),
            dma((3 * CHUNKS,)),
            dma((32,)),
            dma((32,)),
            dma((PARTS * 64,)),
            dma((PARTS * 64,)),
            dma((PARTS * 4,)),
            dma((PARTS * 4,)),
            dma((2,)),
        ],
        compiler_params=pltpu.CompilerParams(
            collective_id=0, has_side_effects=True, vmem_limit_bytes=56 * 2**20
        ),
    )(
        hist_x.reshape(ROWS, D), hist_len, cand_x, cand_user.reshape(1, CAND), w_proj, w_out,
        norm_gain.reshape(1, D),
    )
    tiles = 4
    each = tiles // PARTS
    hist_out, cand_out = pl.pallas_call(
        last_kernel,
        grid=(tiles,),
        out_shape=(jax.ShapeDtypeStruct((ROWS, D), BF), jax.ShapeDtypeStruct((CAND, D), BF)),
        in_specs=[
            pl.BlockSpec((CAND, CAND), lambda n: (0, 0)),
            pl.BlockSpec((CAND, QUARTER), lambda n: (n // each, n % each)),
            pl.BlockSpec((ROWS, QUARTER), lambda n: (0, n)),
        ],
        out_specs=(
            pl.BlockSpec((ROWS, QUARTER), lambda n: (0, n)),
            pl.BlockSpec((CAND, QUARTER), lambda n: (0, n)),
        ),
    )(unsort, sorted_rows, hist_rows)
    return hist_out[None], cand_out


def solution(mesh):
    in_specs = (P("cand", "seq", None), P(), P("cand", None), P("cand", None), P(), P(), P())
    out_specs = (P("cand", "seq", None), P("cand", None))
    return jax.shard_map(
        per_device, mesh=mesh, in_specs=in_specs, out_specs=out_specs, check_vma=False
    )
```

```python
import jax
import jax.numpy as jnp
from jax import lax
from jax.experimental import pallas as pl
from jax.experimental.pallas import tpu as pltpu
from jax.sharding import PartitionSpec as P


HEADS = 8
HEAD = 128
D = 1024
ROWS = 128
CHUNKS = 4
CROWS = ROWS // CHUNKS
CAND = 512
QUARTER = 256
PARTS = 2
WIDE = D // PARTS
PIECE = WIDE // 4
MESH = pl.DeviceIdType.MESH
BF = jnp.bfloat16
F32 = jnp.float32
I32 = jnp.int32
NT = (((1,), (1,)), ((), ()))


def silu(a):
    half = 0.5 * a
    return half + half * jnp.tanh(half)


def iota(shape, dim):
    return lax.broadcasted_iota(I32, shape, dim)


def onehot(condition):
    return jnp.where(condition, 1.0, 0.0).astype(BF)


def dot(a, b):
    return jnp.dot(a, b, preferred_element_type=F32)


def remote(src, dst, send, recv, seq, cand):
    return pltpu.make_async_remote_copy(
        src_ref=src, dst_ref=dst, send_sem=send, recv_sem=recv,
        device_id={"seq": seq, "cand": cand}, device_id_type=MESH,
    )


def kernel(
    x_hbm, len_ref, candx_hbm, cuser_ref, wp_hbm, wo_hbm, gain_ref,
    hist_ref, sorted_rows, order_ref,
    wp, wo, candx, xb, keys, values, xc, xh, qg, acc, normed_ref, msgs, rdisp, back, rret, crep, picked_rows, hist_tmp,
    load_sem, swap_send, swap_recv, x_send, x_recv, fwd_send, d_send, d_recv, r_send, r_recv, g_send, g_recv, h_sem,
):
    s = lax.axis_index("seq")
    c = lax.axis_index("cand")
    x, zh = s // 2, s % 2
    core, y, zl = c % 2, (c // 2) % 4, c // 8
    z = zh * 4 + zl
    user = c - core + zh
    other_core = c + 1 - 2 * core
    early = core == zh
    late = core != zh
    swap_seq = 2 * x + core

    barrier = pltpu.get_barrier_semaphore()

    def greet(i, carry):
        pl.semaphore_signal(
            barrier, inc=1, device_id={"seq": 2 * x + ((zh + (i >> 5)) & 1), "cand": (c + i) & 31}, device_id_type=MESH
        )
        return carry

    lax.fori_loop(1, 64, greet, 0)
    for i in range(1, 4):
        pl.semaphore_signal(
            barrier, inc=1, device_id={"seq": 2 * ((x + i) % 4) + zh, "cand": c}, device_id_type=MESH
        )

    def load(src, dst, i):
        return pltpu.make_async_copy(src, dst, load_sem.at[i])

    def slot_rows(kind, there, j):
        return xb.at[pl.ds(pl.multiple_of(kind * 4 * ROWS + j * ROWS + there * CROWS, CROWS), CROWS)]

    def own_load(j):
        return load(x_hbm.at[pl.ds(j * CROWS, CROWS)], slot_rows(core, x, j), 3 + j)

    cand_load = load(candx_hbm, candx, 0)
    wp_load = load(wp_hbm, wp, 1)
    wo_load = load(wo_hbm, wo, 2)

    @pl.when(early)
    def _():
        for j in range(CHUNKS):
            own_load(j).start()

    cand_load.start()

    @pl.when(early)
    def _():
        for j in range(CHUNKS):
            own_load(j).wait()

    pl.semaphore_wait(barrier, 66)

    def swap_copy(j):
        return remote(
            x_hbm.at[pl.ds(j * CROWS, CROWS)], slot_rows(zh, x, j), swap_send.at[j], swap_recv.at[j], swap_seq, user
        )

    def own_copy(i, j):
        rows = slot_rows(core, x, j)
        recv = x_recv.at[(core * 4 + x) * CHUNKS + j]
        if i == 0:
            return remote(rows, rows, x_send.at[j], recv, s, other_core)
        return remote(rows, rows, x_send.at[i * CHUNKS + j], recv, 2 * ((x + i) % 4) + zh, c)

    def slot_wait(kind, there, j):
        rows = slot_rows(kind, there, j)
        recv = x_recv.at[(kind * 4 + there) * CHUNKS + j]
        remote(rows, rows, fwd_send.at[0], recv, s, other_core).wait_recv()

    def fwd_copy(i, j):
        there = (x + i) % 4
        rows = slot_rows(core, there, j)
        recv = x_recv.at[(core * 4 + there) * CHUNKS + j]
        return remote(rows, rows, fwd_send.at[(i - 1) * CHUNKS + j], recv, s, other_core)

    def send_own(j):
        for i in range(4):
            own_copy(i, j).start()

    def forward(j):
        for i in range(1, 4):
            slot_wait(core, (x + i) % 4, j)
            fwd_copy(i, j).start()

    def take(j):
        for i in range(4):
            slot_wait(1 - core, (x + i) % 4, j)

    @pl.when(late)
    def _():
        for j in range(CHUNKS):
            swap_copy(j).start()

    @pl.when(early)
    def _():
        for j in range(CHUNKS):
            send_own(j)

    wp_load.start()
    wo_load.start()

    owner = cuser_ref[...]
    is_user = owner == iota((32, CAND), 0)
    users = onehot(is_user)
    before = dot(users, onehot(iota((CAND, CAND), 0) < iota((CAND, CAND), 1)))
    within = jnp.sum(jnp.where(is_user, before, 0.0), axis=0, keepdims=True).astype(I32)
    smaller = dot(onehot(iota((32, 32), 1) < iota((32, 32), 0)), users)
    start = jnp.sum(smaller, axis=1, keepdims=True)
    place = jnp.sum(jnp.where(is_user, start, 0.0), axis=0, keepdims=True).astype(I32) + within
    part = place & 7
    code = owner * 32 + part * 4 + (within >> 3)
    sorted_at = ((part >> 1) << 7) + ((part & 1) << 6) + (place >> 3)

    def message(m):
        which, dy = m >> 2, m & 3
        pair = which >> 1
        dz = jnp.where(
            pair == 0, 0, jnp.where(pair == 1, 1, jnp.where(pair == 2, 7, jnp.where(which == 6, 2, 6)))
        )
        dcore = which & 1
        tz = (z + dz) & 7
        ty = (y + dy) & 3
        tcore = (core + dcore) & 1
        column = (tz & 3) * 4 + ty
        return column * 2 + (tz >> 2), tz >> 2, column * 2 + tcore, tcore

    slot = iota((CAND, 1), 0)
    to_user, _, _, to_core = message(slot >> 4)
    slot_code = to_user * 32 + (2 * x + to_core) * 4 + (slot & 3)
    match = slot_code == code
    slot_quarter = (slot >> 2) & 3
    cand_load.wait()
    sent = jnp.zeros((CAND, QUARTER), F32)
    for j in range(4):
        sent += dot(onehot(match & (slot_quarter == j)), candx[:, j * QUARTER : (j + 1) * QUARTER])
    msgs[...] = sent.astype(BF)

    def piece(ref, i):
        return ref.at[pl.ds(pl.multiple_of(i * 16, 16), 16)]

    def d_copy(m):
        _, tzh, tcand, _ = message(m)
        return remote(piece(msgs, m), piece(rdisp, c), d_send.at[0], d_recv.at[0], 2 * x + tzh, tcand)

    self_d = pltpu.make_async_copy(piece(msgs, 0), piece(rdisp, c), d_recv.at[0])
    self_d.start()

    def send_d(m, carry):
        d_copy(m).start()
        return carry

    lax.fori_loop(1, 32, send_d, 0)

    length = len_ref[user]

    def block_pos(kind, row):
        return (2 * ((row >> 5) & 3) + kind) * ROWS + (row >> 7) * CROWS + (row & (CROWS - 1))

    def project(kind, first, count):
        rows = pl.ds(pl.multiple_of((kind * 4 + first) * ROWS, ROWS), count * ROWS)
        alive = block_pos(kind, first * ROWS + iota((count * ROWS, 1), 0)) < length

        def step(n, carry):
            cols = pl.ds(pl.multiple_of(n * QUARTER, QUARTER), QUARTER)
            kcols = pl.ds(pl.multiple_of(3 * D + n * QUARTER, QUARTER), QUARTER)
            vcols = pl.ds(pl.multiple_of(D + n * QUARTER, QUARTER), QUARTER)
            keys[rows, cols] = silu(dot(xb[rows, :], wp[:, kcols])).astype(BF)
            values[rows, cols] = jnp.where(alive, silu(dot(xb[rows, :], wp[:, vcols])), 0.0).astype(BF)
            return carry

        lax.fori_loop(0, 4, step, 0, unroll=2)

    def project_q(rows_ref):
        def step(n, carry):
            cols = pl.ds(pl.multiple_of(n * QUARTER, QUARTER), QUARTER)
            qcols = pl.ds(pl.multiple_of(D + n * QUARTER, QUARTER), QUARTER)
            wcols = pl.ds(pl.multiple_of(2 * D + n * QUARTER, QUARTER), QUARTER)
            qg[:, qcols] = silu(dot(rows_ref[...], wp[:, wcols])).astype(BF)
            qg[:, cols] = silu(dot(rows_ref[...], wp[:, cols])).astype(BF)
            return carry

        lax.fori_loop(0, 4, step, 0, unroll=2)

    def attend(top, count, allowed, first):
        rows = pl.ds(top, count)
        for h in range(HEADS):
            cols = slice(h * HEAD, (h + 1) * HEAD)
            scores = lax.dot_general(
                qg[:, D + h * HEAD : D + (h + 1) * HEAD], keys[rows, cols], NT, preferred_element_type=F32
            )
            weights = silu(scores * HEAD ** -0.5)
            if allowed is not None:
                weights = jnp.where(allowed, weights, 0.0)
            mixed = dot(weights.astype(BF), values[rows, cols])
            if first:
                acc[:, cols] = mixed
            else:
                acc[:, cols] += mixed

    def pair_top(kind, pair):
        return pl.multiple_of((kind * 2 + pair) * 2 * ROWS, 2 * ROWS)

    wp_load.wait()
    for j in range(CHUNKS):
        @pl.when(late)
        def _():
            swap_copy(j).wait_recv()
            send_own(j)
            take(j)

        @pl.when(early)
        def _():
            forward(j)

        project(zh, j, 1)

    def late_forward(j):
        @pl.when(late)
        def _():
            forward(j)

    def early_take(j):
        @pl.when(early)
        def _():
            take(j)

    late_forward(0)

    pltpu.make_async_copy(rdisp, rdisp, d_recv.at[0]).wait()
    here = iota((ROWS, CAND), 0)
    lane = iota((ROWS, CAND), 1)
    same = ((here >> 2) == (lane >> 4)) & ((here & 3) == (lane & 3))
    lane_quarter = (lane >> 2) & 3
    for j in range(4):
        xc[:, j * QUARTER : (j + 1) * QUARTER] = dot(onehot(same & (lane_quarter == j)), rdisp[...]).astype(BF)
    project_q(xc)
    late_forward(1)
    attend(pair_top(zh, 0), 4 * ROWS, None, True)
    late_forward(2)
    late_forward(3)
    early_take(0)
    early_take(1)
    project(1 - zh, 0, 2)
    attend(pair_top(1 - zh, 0), 2 * ROWS, None, False)
    early_take(2)
    early_take(3)
    project(1 - zh, 2, 2)
    attend(pair_top(1 - zh, 1), 2 * ROWS, None, False)
    wo_load.wait()

    def normalise():
        totals = acc[...]
        average = jnp.mean(totals, axis=1, keepdims=True)
        centred = totals - average
        variance = jnp.mean(centred * centred, axis=1, keepdims=True)
        normed_ref[...] = (
            centred * lax.rsqrt(variance + 1e-05) * gain_ref[...] * qg[:, 0:D].astype(F32)
        ).astype(BF)

    def finish(rows_ref, cols):
        return (dot(normed_ref[...], wo[:, cols]) + rows_ref[:, cols].astype(F32)).astype(BF)

    normalise()
    tall = iota((CAND, ROWS), 0)
    wide = iota((CAND, ROWS), 1)
    same_t = ((wide >> 2) == (tall >> 4)) & ((wide & 3) == (tall & 3))
    tall_quarter = (tall >> 2) & 3
    my_ret = user * 2 + core

    def r_copy(i, part):
        there = (c + i) & 31
        return remote(
            piece(back, part * 32 + there), piece(rret, part * 64 + my_ret), r_send.at[part],
            r_recv.at[part], 2 * x + ((zh + (i >> 5)) & 1), there,
        )

    def self_r(part):
        return pltpu.make_async_copy(
            piece(back, part * 32 + c), piece(rret, part * 64 + my_ret), r_recv.at[part]
        )

    for part in range(PARTS):
        done = finish(xc, slice(part * WIDE, (part + 1) * WIDE))
        returned = jnp.zeros((CAND, PIECE), F32)
        for j in range(4):
            returned += dot(onehot(same_t & (tall_quarter == j)), done[:, j * PIECE : (j + 1) * PIECE])
        back[part * CAND : (part + 1) * CAND, :] = returned.astype(BF)
        self_r(part).start()

        def send_r(i, carry):
            r_copy(i, part).start()
            return carry

        lax.fori_loop(1, 64, send_r, 0, unroll=7)

    ret = iota((1024, 1), 0)
    ret_to = ret >> 4
    ret_code = (ret_to >> 1) * 32 + (2 * x + (ret_to & 1)) * 4 + (ret & 3)
    mine = iota((ROWS, 1), 0)
    mine_place = 8 * (mine & 63) + 2 * x + (mine >> 6)
    places = lax.dot_general(
        onehot(mine_place == place), onehot(ret_code == code), NT, preferred_element_type=F32
    )
    ret_quarter = (iota((ROWS, 1024), 1) >> 2) & 3
    for j in range(4):
        crep[j * ROWS : (j + 1) * ROWS, :] = jnp.where(ret_quarter == j, places, 0.0).astype(BF)
    order_ref[...] = sorted_at

    for j in range(CHUNKS):
        xh[j * CROWS : (j + 1) * CROWS, :] = slot_rows(core, x, j)[...]
    project_q(xh)
    query_pos = (2 * x + core) * ROWS + iota((ROWS, 1), 0)
    key = iota((1, 8 * ROWS), 1)
    attend(0, 8 * ROWS, block_pos(key >> 9, key & 511) <= query_pos, True)
    normalise()
    hist_tmp[...] = finish(xh, slice(0, D))
    hist_copy = remote(hist_tmp, hist_ref, h_sem.at[0], h_sem.at[1], swap_seq, user)

    hist_home = pltpu.make_async_copy(hist_tmp, hist_ref, h_sem.at[0])

    @pl.when(early)
    def _():
        hist_home.start()

    def sorted_part(part, there):
        return sorted_rows.at[pl.ds(pl.multiple_of(part * CAND + there * ROWS, ROWS), ROWS)]

    def picked_part(part):
        return picked_rows.at[part * ROWS : (part + 1) * ROWS]

    def g_home(part):
        return pltpu.make_async_copy(picked_part(part), sorted_part(part, x), g_send.at[part * 4])

    def g_copy(i, part):
        return remote(
            picked_part(part), sorted_part(part, x), g_send.at[part * 4 + i], g_recv.at[part * 4 + x], 2 * ((x + i) % 4) + zh, c
        )

    for part in range(PARTS):
        arrived = rret.at[part * 1024 : (part + 1) * 1024]
        pltpu.make_async_copy(arrived, arrived, r_recv.at[part]).wait()
        picked = dot(crep[...], rret[part * 1024 : (part + 1) * 1024, :]).astype(BF)
        for j in range(4):
            picked_rows[part * ROWS : (part + 1) * ROWS, j * PIECE : (j + 1) * PIECE] = picked[
                j * ROWS : (j + 1) * ROWS, :
            ]
        for i in range(1, 4):
            g_copy(i, part).start()
        g_home(part).start()

    @pl.when(late)
    def _():
        hist_copy.start()

    for part in range(PARTS):
        for i in range(1, 4):
            from_x = (x + i) % 4
            rows = sorted_part(part, from_x)
            remote(rows, rows, g_send.at[0], g_recv.at[part * 4 + from_x], s, other_core).wait_recv()

    for part in range(PARTS):
        for i in range(1, 4):
            g_copy(i, part).wait_send()
        g_home(part).wait()

        gone = rret.at[pl.ds(part * 1024, 63 * 16)]
        remote(gone, gone, r_send.at[part], r_recv.at[part], s, other_core).wait_send()

    left = rdisp.at[pl.ds(0, 31 * 16)]
    remote(left, left, d_send.at[0], d_recv.at[0], s, other_core).wait_send()
    for j in range(CHUNKS):
        for i in range(4):
            own_copy(i, j).wait_send()
        for i in range(1, 4):
            fwd_copy(i, j).wait_send()

    @pl.when(late)
    def _():
        for j in range(CHUNKS):
            swap_copy(j).wait_send()
        hist_copy.wait()

    @pl.when(early)
    def _():
        hist_home.wait()


def last_kernel(order_ref, rows_hbm, hist_hbm, hist_ref, cand_ref, rows, out, hist, load_sem, store_sem):
    hist_load = pltpu.make_async_copy(hist_hbm, hist, load_sem.at[4])
    hist_load.start()
    loads, stores = [], []
    for n in range(4):
        part, first = n * QUARTER // WIDE, n * QUARTER % WIDE
        src = rows_hbm.at[pl.ds(part * CAND, CAND), pl.ds(first, QUARTER)]
        loads.append(pltpu.make_async_copy(src, rows.at[n], load_sem.at[n]))
        loads[n].start()
    unsort = lax.dot_general(
        onehot(iota((CAND, CAND), 0) == iota((CAND, CAND), 1)),
        onehot(iota((CAND, 1), 0) == order_ref[...]), NT, preferred_element_type=F32,
    ).astype(BF)
    for n in range(4):
        loads[n].wait()
        out[n] = dot(unsort, rows[n]).astype(BF)
        stores.append(
            pltpu.make_async_copy(out.at[n], cand_ref.at[:, pl.ds(n * QUARTER, QUARTER)], store_sem.at[n])
        )
        stores[-1].start()
        if n == 0:
            hist_load.wait()
            stores.append(pltpu.make_async_copy(hist, hist_ref, store_sem.at[4]))
            stores[1].start()
    for store in stores:
        store.wait()


def per_device(hist_x, hist_len, cand_x, cand_user, w_proj, w_out, norm_gain):
    any_spec = pl.BlockSpec(memory_space=pl.ANY)
    vmem = pl.BlockSpec(memory_space=pltpu.VMEM)
    dma = pltpu.SemaphoreType.DMA
    hist_rows, sorted_rows, order = pl.pallas_call(
        kernel,
        out_shape=(
            jax.ShapeDtypeStruct((ROWS, D), BF),
            jax.ShapeDtypeStruct((PARTS * CAND, WIDE), BF),
            jax.ShapeDtypeStruct((1, CAND), I32),
        ),
        in_specs=[any_spec, pl.BlockSpec(memory_space=pltpu.SMEM), any_spec, vmem, any_spec, any_spec, vmem],
        out_specs=(any_spec, any_spec, vmem),
        scratch_shapes=[
            pltpu.VMEM((D, 4 * D), BF),
            pltpu.VMEM((D, D), BF),
            pltpu.VMEM((CAND, D), BF),
            pltpu.VMEM((8 * ROWS, D), BF),
            pltpu.VMEM((8 * ROWS, D), BF),
            pltpu.VMEM((8 * ROWS, D), BF),
            pltpu.VMEM((ROWS, D), BF),
            pltpu.VMEM((ROWS, D), BF),
            pltpu.VMEM((ROWS, 2 * D), BF),
            pltpu.VMEM((ROWS, D), F32),
            pltpu.VMEM((ROWS, D), BF),
            pltpu.VMEM((CAND, QUARTER), BF),
            pltpu.VMEM((CAND, QUARTER), BF),
            pltpu.VMEM((PARTS * CAND, PIECE), BF),
            pltpu.VMEM((2 * PARTS * CAND, PIECE), BF),
            pltpu.VMEM((4 * ROWS, 2 * CAND), BF),
            pltpu.VMEM((PARTS * ROWS, WIDE), BF),
            pltpu.VMEM((ROWS, D), BF),
            dma((3 + CHUNKS,)),
            dma((CHUNKS,)),
            dma((CHUNKS,)),
            dma((4 * CHUNKS,)),
            dma((8 * CHUNKS,)),
            dma((3 * CHUNKS,)),
            dma((1,)),
            dma((1,)),
            dma((PARTS,)),
            dma((PARTS,)),
            dma((PARTS * 4,)),
            dma((PARTS * 4,)),
            dma((2,)),
        ],
        compiler_params=pltpu.CompilerParams(
            collective_id=0, has_side_effects=True, vmem_limit_bytes=56 * 2**20
        ),
    )(
        hist_x.reshape(ROWS, D), hist_len, cand_x, cand_user.reshape(1, CAND), w_proj, w_out,
        norm_gain.reshape(1, D),
    )
    hist_out, cand_out = pl.pallas_call(
        last_kernel,
        out_shape=(jax.ShapeDtypeStruct((ROWS, D), BF), jax.ShapeDtypeStruct((CAND, D), BF)),
        in_specs=[vmem, any_spec, any_spec],
        out_specs=(any_spec, any_spec),
        scratch_shapes=[
            pltpu.VMEM((4, CAND, QUARTER), BF),
            pltpu.VMEM((4, CAND, QUARTER), BF),
            pltpu.VMEM((ROWS, D), BF),
            dma((5,)),
            dma((5,)),
        ],
        compiler_params=pltpu.CompilerParams(vmem_limit_bytes=56 * 2**20),
    )(order, sorted_rows, hist_rows)
    return hist_out[None], cand_out


def solution(mesh):
    in_specs = (P("cand", "seq", None), P(), P("cand", None), P("cand", None), P(), P(), P())
    out_specs = (P("cand", "seq", None), P("cand", None))
    return jax.shard_map(
        per_device, mesh=mesh, in_specs=in_specs, out_specs=out_specs, check_vma=False
    )
```

```python
import jax
import jax.numpy as jnp
from jax import lax
from jax.experimental import pallas as pl
from jax.experimental.pallas import tpu as pltpu
from jax.sharding import PartitionSpec as P


HEADS = 8
HEAD = 128
D = 1024
ROWS = 128
CHUNKS = 4
CROWS = ROWS // CHUNKS
CAND = 512
QUARTER = 256
PARTS = 2
WIDE = D // PARTS
PIECE = WIDE // 4
MESH = pl.DeviceIdType.MESH
BF = jnp.bfloat16
F32 = jnp.float32
I32 = jnp.int32
NT = (((1,), (1,)), ((), ()))


def silu(a):
    half = 0.5 * a
    return half + half * jnp.tanh(half)


def iota(shape, dim):
    return lax.broadcasted_iota(I32, shape, dim)


def onehot(condition):
    return jnp.where(condition, 1.0, 0.0).astype(BF)


def dot(a, b):
    return jnp.dot(a, b, preferred_element_type=F32)


def remote(src, dst, send, recv, seq, cand):
    return pltpu.make_async_remote_copy(
        src_ref=src, dst_ref=dst, send_sem=send, recv_sem=recv,
        device_id={"seq": seq, "cand": cand}, device_id_type=MESH,
    )


def kernel(
    x_hbm, len_ref, candx_hbm, cuser_ref, wp_hbm, wo_hbm, gain_ref,
    hist_ref, sorted_rows, order_ref,
    wp, wo, candx, xb, keys, values, xc, xh, qg, acc, normed_ref, msgs, rdisp, back, rret, crep, picked_rows, hist_tmp,
    load_sem, swap_send, swap_recv, x_send, x_recv, fwd_send, d_send, d_recv, r_send, r_recv, g_send, g_recv, h_sem,
):
    s = lax.axis_index("seq")
    c = lax.axis_index("cand")
    x, zh = s // 2, s % 2
    core, y, zl = c % 2, (c // 2) % 4, c // 8
    z = zh * 4 + zl
    user = c - core + zh
    other_core = c + 1 - 2 * core
    early = core == zh
    late = core != zh
    swap_seq = 2 * x + core

    barrier = pltpu.get_barrier_semaphore()

    def greet(i, carry):
        pl.semaphore_signal(
            barrier, inc=1, device_id={"seq": 2 * x + ((zh + (i >> 5)) & 1), "cand": (c + i) & 31}, device_id_type=MESH
        )
        return carry

    lax.fori_loop(1, 64, greet, 0)
    for i in range(1, 4):
        pl.semaphore_signal(
            barrier, inc=1, device_id={"seq": 2 * ((x + i) % 4) + zh, "cand": c}, device_id_type=MESH
        )

    def load(src, dst, i):
        return pltpu.make_async_copy(src, dst, load_sem.at[i])

    def slot_rows(kind, there, j):
        return xb.at[pl.ds(pl.multiple_of(kind * 4 * ROWS + j * ROWS + there * CROWS, CROWS), CROWS)]

    def own_load(j):
        return load(x_hbm.at[pl.ds(j * CROWS, CROWS)], slot_rows(core, x, j), 3 + j)

    cand_load = load(candx_hbm, candx, 0)
    wp_load = load(wp_hbm, wp, 1)
    wo_load = load(wo_hbm, wo, 2)

    @pl.when(early)
    def _():
        for j in range(CHUNKS):
            own_load(j).start()

    cand_load.start()

    @pl.when(early)
    def _():
        for j in range(CHUNKS):
            own_load(j).wait()

    pl.semaphore_wait(barrier, 66)

    def swap_copy(j):
        return remote(
            x_hbm.at[pl.ds(j * CROWS, CROWS)], slot_rows(zh, x, j), swap_send.at[j], swap_recv.at[j], swap_seq, user
        )

    def own_copy(i, j):
        rows = slot_rows(core, x, j)
        recv = x_recv.at[(core * 4 + x) * CHUNKS + j]
        if i == 0:
            return remote(rows, rows, x_send.at[j], recv, s, other_core)
        return remote(rows, rows, x_send.at[i * CHUNKS + j], recv, 2 * ((x + i) % 4) + zh, c)

    def slot_wait(kind, there, j):
        rows = slot_rows(kind, there, j)
        recv = x_recv.at[(kind * 4 + there) * CHUNKS + j]
        remote(rows, rows, fwd_send.at[0], recv, s, other_core).wait_recv()

    def fwd_copy(i, j):
        there = (x + i) % 4
        rows = slot_rows(core, there, j)
        recv = x_recv.at[(core * 4 + there) * CHUNKS + j]
        return remote(rows, rows, fwd_send.at[(i - 1) * CHUNKS + j], recv, s, other_core)

    def send_own(j):
        for i in range(4):
            own_copy(i, j).start()

    def forward(j):
        for i in range(1, 4):
            slot_wait(core, (x + i) % 4, j)
            fwd_copy(i, j).start()

    def take(j):
        for i in range(4):
            slot_wait(1 - core, (x + i) % 4, j)

    @pl.when(late)
    def _():
        for j in range(CHUNKS):
            swap_copy(j).start()

    @pl.when(early)
    def _():
        for j in range(CHUNKS):
            send_own(j)

    wp_load.start()
    wo_load.start()

    owner = cuser_ref[...]
    is_user = owner == iota((32, CAND), 0)
    users = onehot(is_user)
    before = dot(users, onehot(iota((CAND, CAND), 0) < iota((CAND, CAND), 1)))
    within = jnp.sum(jnp.where(is_user, before, 0.0), axis=0, keepdims=True).astype(I32)
    smaller = dot(onehot(iota((32, 32), 1) < iota((32, 32), 0)), users)
    start = jnp.sum(smaller, axis=1, keepdims=True)
    place = jnp.sum(jnp.where(is_user, start, 0.0), axis=0, keepdims=True).astype(I32) + within
    part = place & 7
    code = owner * 32 + part * 4 + (within >> 3)
    sorted_at = ((part >> 1) << 7) + ((part & 1) << 6) + (place >> 3)

    def message(m):
        which, dy = m >> 2, m & 3
        pair = which >> 1
        dz = jnp.where(
            pair == 0, 0, jnp.where(pair == 1, 1, jnp.where(pair == 2, 7, jnp.where(which == 6, 2, 6)))
        )
        dcore = which & 1
        tz = (z + dz) & 7
        ty = (y + dy) & 3
        tcore = (core + dcore) & 1
        column = (tz & 3) * 4 + ty
        return column * 2 + (tz >> 2), tz >> 2, column * 2 + tcore, tcore

    slot = iota((CAND, 1), 0)
    to_user, _, _, to_core = message(slot >> 4)
    slot_code = to_user * 32 + (2 * x + to_core) * 4 + (slot & 3)
    match = slot_code == code
    slot_quarter = (slot >> 2) & 3
    cand_load.wait()
    sent = jnp.zeros((CAND, QUARTER), F32)
    for j in range(4):
        sent += dot(onehot(match & (slot_quarter == j)), candx[:, j * QUARTER : (j + 1) * QUARTER])
    msgs[...] = sent.astype(BF)

    def piece(ref, i):
        return ref.at[pl.ds(pl.multiple_of(i * 16, 16), 16)]

    def d_copy(m):
        _, tzh, tcand, _ = message(m)
        return remote(piece(msgs, m), piece(rdisp, c), d_send.at[0], d_recv.at[0], 2 * x + tzh, tcand)

    self_d = pltpu.make_async_copy(piece(msgs, 0), piece(rdisp, c), d_recv.at[0])
    self_d.start()

    def send_d(m, carry):
        d_copy(m).start()
        return carry

    lax.fori_loop(1, 32, send_d, 0)

    length = len_ref[user]

    def block_pos(kind, row):
        return (2 * ((row >> 5) & 3) + kind) * ROWS + (row >> 7) * CROWS + (row & (CROWS - 1))

    def project(kind, first, count):
        rows = pl.ds(pl.multiple_of((kind * 4 + first) * ROWS, ROWS), count * ROWS)
        alive = block_pos(kind, first * ROWS + iota((count * ROWS, 1), 0)) < length

        def step(n, carry):
            cols = pl.ds(pl.multiple_of(n * QUARTER, QUARTER), QUARTER)
            kcols = pl.ds(pl.multiple_of(3 * D + n * QUARTER, QUARTER), QUARTER)
            vcols = pl.ds(pl.multiple_of(D + n * QUARTER, QUARTER), QUARTER)
            keys[rows, cols] = silu(dot(xb[rows, :], wp[:, kcols])).astype(BF)
            values[rows, cols] = jnp.where(alive, silu(dot(xb[rows, :], wp[:, vcols])), 0.0).astype(BF)
            return carry

        lax.fori_loop(0, 4, step, 0, unroll=2)

    def project_q(rows_ref):
        def step(n, carry):
            cols = pl.ds(pl.multiple_of(n * QUARTER, QUARTER), QUARTER)
            qcols = pl.ds(pl.multiple_of(D + n * QUARTER, QUARTER), QUARTER)
            wcols = pl.ds(pl.multiple_of(2 * D + n * QUARTER, QUARTER), QUARTER)
            qg[:, qcols] = silu(dot(rows_ref[...], wp[:, wcols])).astype(BF)
            qg[:, cols] = silu(dot(rows_ref[...], wp[:, cols])).astype(BF)
            return carry

        lax.fori_loop(0, 4, step, 0, unroll=2)

    def attend(top, count, allowed, first):
        rows = pl.ds(top, count)
        for h in range(HEADS):
            cols = slice(h * HEAD, (h + 1) * HEAD)
            scores = lax.dot_general(
                qg[:, D + h * HEAD : D + (h + 1) * HEAD], keys[rows, cols], NT, preferred_element_type=F32
            )
            weights = silu(scores * HEAD ** -0.5)
            if allowed is not None:
                weights = jnp.where(allowed, weights, 0.0)
            mixed = dot(weights.astype(BF), values[rows, cols])
            if first:
                acc[:, cols] = mixed
            else:
                acc[:, cols] += mixed

    def pair_top(kind, pair):
        return pl.multiple_of((kind * 2 + pair) * 2 * ROWS, 2 * ROWS)

    wp_load.wait()
    for j in range(CHUNKS):
        @pl.when(late)
        def _():
            swap_copy(j).wait_recv()
            send_own(j)
            take(j)

        @pl.when(early)
        def _():
            forward(j)

        project(zh, j, 1)

    def late_forward(j):
        @pl.when(late)
        def _():
            forward(j)

    def early_take(j):
        @pl.when(early)
        def _():
            take(j)

    late_forward(0)

    pltpu.make_async_copy(rdisp, rdisp, d_recv.at[0]).wait()
    here = iota((ROWS, CAND), 0)
    lane = iota((ROWS, CAND), 1)
    same = ((here >> 2) == (lane >> 4)) & ((here & 3) == (lane & 3))
    lane_quarter = (lane >> 2) & 3
    for j in range(4):
        xc[:, j * QUARTER : (j + 1) * QUARTER] = dot(onehot(same & (lane_quarter == j)), rdisp[...]).astype(BF)
    project_q(xc)
    late_forward(1)
    attend(pair_top(zh, 0), 4 * ROWS, None, True)
    late_forward(2)
    late_forward(3)
    early_take(0)
    early_take(1)
    project(1 - zh, 0, 2)
    attend(pair_top(1 - zh, 0), 2 * ROWS, None, False)
    early_take(2)
    early_take(3)
    project(1 - zh, 2, 2)
    attend(pair_top(1 - zh, 1), 2 * ROWS, None, False)
    wo_load.wait()

    def normalise():
        totals = acc[...]
        average = jnp.mean(totals, axis=1, keepdims=True)
        centred = totals - average
        variance = jnp.mean(centred * centred, axis=1, keepdims=True)
        normed_ref[...] = (
            centred * lax.rsqrt(variance + 1e-05) * gain_ref[...] * qg[:, 0:D].astype(F32)
        ).astype(BF)

    def finish(rows_ref, cols):
        return (dot(normed_ref[...], wo[:, cols]) + rows_ref[:, cols].astype(F32)).astype(BF)

    normalise()
    tall = iota((CAND, ROWS), 0)
    wide = iota((CAND, ROWS), 1)
    same_t = ((wide >> 2) == (tall >> 4)) & ((wide & 3) == (tall & 3))
    tall_quarter = (tall >> 2) & 3
    my_ret = user * 2 + core

    def r_copy(i, part):
        there = (c + i) & 31
        return remote(
            piece(back, part * 32 + there), piece(rret, part * 64 + my_ret), r_send.at[part],
            r_recv.at[part], 2 * x + ((zh + (i >> 5)) & 1), there,
        )

    def self_r(part):
        return pltpu.make_async_copy(
            piece(back, part * 32 + c), piece(rret, part * 64 + my_ret), r_recv.at[part]
        )

    for part in range(PARTS):
        done = finish(xc, slice(part * WIDE, (part + 1) * WIDE))
        returned = jnp.zeros((CAND, PIECE), F32)
        for j in range(4):
            returned += dot(onehot(same_t & (tall_quarter == j)), done[:, j * PIECE : (j + 1) * PIECE])
        back[part * CAND : (part + 1) * CAND, :] = returned.astype(BF)
        self_r(part).start()

        def send_r(i, carry):
            r_copy(i, part).start()
            return carry

        lax.fori_loop(1, 64, send_r, 0, unroll=7)

    ret = iota((1024, 1), 0)
    ret_to = ret >> 4
    ret_code = (ret_to >> 1) * 32 + (2 * x + (ret_to & 1)) * 4 + (ret & 3)
    mine = iota((ROWS, 1), 0)
    mine_place = 8 * (mine & 63) + 2 * x + (mine >> 6)
    places = lax.dot_general(
        onehot(mine_place == place), onehot(ret_code == code), NT, preferred_element_type=F32
    )
    ret_quarter = (iota((ROWS, 1024), 1) >> 2) & 3
    for j in range(4):
        crep[j * ROWS : (j + 1) * ROWS, :] = jnp.where(ret_quarter == j, places, 0.0).astype(BF)
    order_ref[...] = sorted_at

    for j in range(CHUNKS):
        xh[j * CROWS : (j + 1) * CROWS, :] = slot_rows(core, x, j)[...]
    project_q(xh)
    query_pos = (2 * x + core) * ROWS + iota((ROWS, 1), 0)
    key = iota((1, 8 * ROWS), 1)
    attend(0, 8 * ROWS, block_pos(key >> 9, key & 511) <= query_pos, True)
    normalise()
    hist_tmp[...] = finish(xh, slice(0, D))
    hist_copy = remote(hist_tmp, hist_ref, h_sem.at[0], h_sem.at[1], swap_seq, user)

    hist_home = pltpu.make_async_copy(hist_tmp, hist_ref, h_sem.at[0])

    @pl.when(early)
    def _():
        hist_home.start()

    def sorted_part(part, there):
        return sorted_rows.at[pl.ds(pl.multiple_of(part * CAND + there * ROWS, ROWS), ROWS)]

    def picked_part(part):
        return picked_rows.at[part * ROWS : (part + 1) * ROWS]

    def g_home(part):
        return pltpu.make_async_copy(picked_part(part), sorted_part(part, x), g_send.at[part * 4])

    def g_copy(i, part):
        return remote(
            picked_part(part), sorted_part(part, x), g_send.at[part * 4 + i], g_recv.at[part * 4 + x], 2 * ((x + i) % 4) + zh, c
        )

    for part in range(PARTS):
        arrived = rret.at[part * 1024 : (part + 1) * 1024]
        pltpu.make_async_copy(arrived, arrived, r_recv.at[part]).wait()
        picked = dot(crep[...], rret[part * 1024 : (part + 1) * 1024, :]).astype(BF)
        for j in range(4):
            picked_rows[part * ROWS : (part + 1) * ROWS, j * PIECE : (j + 1) * PIECE] = picked[
                j * ROWS : (j + 1) * ROWS, :
            ]
        for i in range(1, 4):
            g_copy(i, part).start()
        g_home(part).start()

    @pl.when(late)
    def _():
        hist_copy.start()

    for part in range(PARTS):
        for i in range(1, 4):
            from_x = (x + i) % 4
            rows = sorted_part(part, from_x)
            remote(rows, rows, g_send.at[0], g_recv.at[part * 4 + from_x], s, other_core).wait_recv()

    for part in range(PARTS):
        for i in range(1, 4):
            g_copy(i, part).wait_send()
        g_home(part).wait()

        gone = rret.at[pl.ds(part * 1024, 63 * 16)]
        remote(gone, gone, r_send.at[part], r_recv.at[part], s, other_core).wait_send()

    left = rdisp.at[pl.ds(0, 31 * 16)]
    remote(left, left, d_send.at[0], d_recv.at[0], s, other_core).wait_send()
    for j in range(CHUNKS):
        for i in range(4):
            own_copy(i, j).wait_send()
        for i in range(1, 4):
            fwd_copy(i, j).wait_send()

    @pl.when(late)
    def _():
        for j in range(CHUNKS):
            swap_copy(j).wait_send()
        hist_copy.wait()

    @pl.when(early)
    def _():
        hist_home.wait()


def last_kernel(order_ref, rows_hbm, hist_hbm, hist_ref, cand_ref, rows, out, hist, load_sem, store_sem):
    hist_load = pltpu.make_async_copy(hist_hbm, hist, load_sem.at[4])
    hist_load.start()
    loads, stores = [], []
    for n in range(PARTS):
        src = rows_hbm.at[pl.ds(n * CAND, CAND)]
        loads.append(pltpu.make_async_copy(src, rows.at[n], load_sem.at[n]))
        loads[n].start()
    unsort = lax.dot_general(
        onehot(iota((CAND, CAND), 0) == iota((CAND, CAND), 1)),
        onehot(iota((CAND, 1), 0) == order_ref[...]), NT, preferred_element_type=F32,
    ).astype(BF)
    for n in range(PARTS):
        loads[n].wait()
        out[n] = dot(unsort, rows[n]).astype(BF)
        stores.append(
            pltpu.make_async_copy(out.at[n], cand_ref.at[:, pl.ds(n * WIDE, WIDE)], store_sem.at[n])
        )
        stores[-1].start()
        if n == 0:
            hist_load.wait()
            stores.append(pltpu.make_async_copy(hist, hist_ref, store_sem.at[4]))
            stores[1].start()
    for store in stores:
        store.wait()


def per_device(hist_x, hist_len, cand_x, cand_user, w_proj, w_out, norm_gain):
    any_spec = pl.BlockSpec(memory_space=pl.ANY)
    vmem = pl.BlockSpec(memory_space=pltpu.VMEM)
    dma = pltpu.SemaphoreType.DMA
    hist_rows, sorted_rows, order = pl.pallas_call(
        kernel,
        out_shape=(
            jax.ShapeDtypeStruct((ROWS, D), BF),
            jax.ShapeDtypeStruct((PARTS * CAND, WIDE), BF),
            jax.ShapeDtypeStruct((1, CAND), I32),
        ),
        in_specs=[any_spec, pl.BlockSpec(memory_space=pltpu.SMEM), any_spec, vmem, any_spec, any_spec, vmem],
        out_specs=(any_spec, any_spec, vmem),
        scratch_shapes=[
            pltpu.VMEM((D, 4 * D), BF),
            pltpu.VMEM((D, D), BF),
            pltpu.VMEM((CAND, D), BF),
            pltpu.VMEM((8 * ROWS, D), BF),
            pltpu.VMEM((8 * ROWS, D), BF),
            pltpu.VMEM((8 * ROWS, D), BF),
            pltpu.VMEM((ROWS, D), BF),
            pltpu.VMEM((ROWS, D), BF),
            pltpu.VMEM((ROWS, 2 * D), BF),
            pltpu.VMEM((ROWS, D), F32),
            pltpu.VMEM((ROWS, D), BF),
            pltpu.VMEM((CAND, QUARTER), BF),
            pltpu.VMEM((CAND, QUARTER), BF),
            pltpu.VMEM((PARTS * CAND, PIECE), BF),
            pltpu.VMEM((2 * PARTS * CAND, PIECE), BF),
            pltpu.VMEM((4 * ROWS, 2 * CAND), BF),
            pltpu.VMEM((PARTS * ROWS, WIDE), BF),
            pltpu.VMEM((ROWS, D), BF),
            dma((3 + CHUNKS,)),
            dma((CHUNKS,)),
            dma((CHUNKS,)),
            dma((4 * CHUNKS,)),
            dma((8 * CHUNKS,)),
            dma((3 * CHUNKS,)),
            dma((1,)),
            dma((1,)),
            dma((PARTS,)),
            dma((PARTS,)),
            dma((PARTS * 4,)),
            dma((PARTS * 4,)),
            dma((2,)),
        ],
        compiler_params=pltpu.CompilerParams(
            collective_id=0, has_side_effects=True, vmem_limit_bytes=56 * 2**20
        ),
    )(
        hist_x.reshape(ROWS, D), hist_len, cand_x, cand_user.reshape(1, CAND), w_proj, w_out,
        norm_gain.reshape(1, D),
    )
    hist_out, cand_out = pl.pallas_call(
        last_kernel,
        out_shape=(jax.ShapeDtypeStruct((ROWS, D), BF), jax.ShapeDtypeStruct((CAND, D), BF)),
        in_specs=[vmem, any_spec, any_spec],
        out_specs=(any_spec, any_spec),
        scratch_shapes=[
            pltpu.VMEM((PARTS, CAND, WIDE), BF),
            pltpu.VMEM((PARTS, CAND, WIDE), BF),
            pltpu.VMEM((ROWS, D), BF),
            dma((5,)),
            dma((5,)),
        ],
        compiler_params=pltpu.CompilerParams(vmem_limit_bytes=56 * 2**20),
    )(order, sorted_rows, hist_rows)
    return hist_out[None], cand_out


def solution(mesh):
    in_specs = (P("cand", "seq", None), P(), P("cand", None), P("cand", None), P(), P(), P())
    out_specs = (P("cand", "seq", None), P("cand", None))
    return jax.shard_map(
        per_device, mesh=mesh, in_specs=in_specs, out_specs=out_specs, check_vma=False
    )
```

```python
import jax
import jax.numpy as jnp
from jax import lax
from jax.experimental import pallas as pl
from jax.experimental.pallas import tpu as pltpu
from jax.sharding import PartitionSpec as P


HEADS = 8
HEAD = 128
D = 1024
ROWS = 128
CHUNKS = 4
CROWS = ROWS // CHUNKS
CAND = 512
QUARTER = 256
PARTS = 2
WIDE = D // PARTS
PIECE = WIDE // 4
MESH = pl.DeviceIdType.MESH
BF = jnp.bfloat16
F32 = jnp.float32
I32 = jnp.int32
NT = (((1,), (1,)), ((), ()))


def silu(a):
    half = 0.5 * a
    return half + half * jnp.tanh(half)


def iota(shape, dim):
    return lax.broadcasted_iota(I32, shape, dim)


def onehot(condition):
    return jnp.where(condition, 1.0, 0.0).astype(BF)


def dot(a, b):
    return jnp.dot(a, b, preferred_element_type=F32)


def remote(src, dst, send, recv, seq, cand):
    return pltpu.make_async_remote_copy(
        src_ref=src, dst_ref=dst, send_sem=send, recv_sem=recv,
        device_id={"seq": seq, "cand": cand}, device_id_type=MESH,
    )


def kernel(
    x_hbm, len_ref, candx_hbm, cuser_ref, wp_hbm, wo_hbm, gain_ref,
    hist_ref, sorted_rows, order_ref,
    wp, wo, candx, xb, keys, values, xc, xh, qg, acc, normed_ref, msgs, rdisp, back, rret, crep, picked_rows, hist_tmp,
    load_sem, swap_send, swap_recv, x_send, x_recv, fwd_send, d_send, d_recv, r_send, r_recv, g_send, g_recv, h_sem,
):
    s = lax.axis_index("seq")
    c = lax.axis_index("cand")
    x, zh = s // 2, s % 2
    core, y, zl = c % 2, (c // 2) % 4, c // 8
    z = zh * 4 + zl
    user = c - core + zh
    other_core = c + 1 - 2 * core
    early = core == zh
    late = core != zh
    swap_seq = 2 * x + core

    barrier = pltpu.get_barrier_semaphore()

    def greet(i, carry):
        pl.semaphore_signal(
            barrier, inc=1, device_id={"seq": 2 * x + ((zh + (i >> 5)) & 1), "cand": (c + i) & 31}, device_id_type=MESH
        )
        return carry

    lax.fori_loop(1, 64, greet, 0)
    for i in range(1, 4):
        pl.semaphore_signal(
            barrier, inc=1, device_id={"seq": 2 * ((x + i) % 4) + zh, "cand": c}, device_id_type=MESH
        )

    def load(src, dst, i):
        return pltpu.make_async_copy(src, dst, load_sem.at[i])

    def slot_rows(kind, there, j):
        return xb.at[pl.ds(pl.multiple_of(kind * 4 * ROWS + j * ROWS + there * CROWS, CROWS), CROWS)]

    def own_load(j):
        return load(x_hbm.at[pl.ds(j * CROWS, CROWS)], slot_rows(core, x, j), 3 + j)

    cand_load = load(candx_hbm, candx, 0)
    wp_load = load(wp_hbm, wp, 1)
    wo_load = load(wo_hbm, wo, 2)

    @pl.when(early)
    def _():
        for j in range(CHUNKS):
            own_load(j).start()

    cand_load.start()

    @pl.when(early)
    def _():
        for j in range(CHUNKS):
            own_load(j).wait()

    pl.semaphore_wait(barrier, 66)

    def swap_copy(j):
        return remote(
            x_hbm.at[pl.ds(j * CROWS, CROWS)], slot_rows(zh, x, j), swap_send.at[j], swap_recv.at[j], swap_seq, user
        )

    def own_copy(i, j):
        rows = slot_rows(core, x, j)
        recv = x_recv.at[(core * 4 + x) * CHUNKS + j]
        if i == 0:
            return remote(rows, rows, x_send.at[j], recv, s, other_core)
        return remote(rows, rows, x_send.at[i * CHUNKS + j], recv, 2 * ((x + i) % 4) + zh, c)

    def slot_wait(kind, there, j):
        rows = slot_rows(kind, there, j)
        recv = x_recv.at[(kind * 4 + there) * CHUNKS + j]
        remote(rows, rows, fwd_send.at[0], recv, s, other_core).wait_recv()

    def fwd_copy(i, j):
        there = (x + i) % 4
        rows = slot_rows(core, there, j)
        recv = x_recv.at[(core * 4 + there) * CHUNKS + j]
        return remote(rows, rows, fwd_send.at[(i - 1) * CHUNKS + j], recv, s, other_core)

    def send_own(j):
        for i in range(4):
            own_copy(i, j).start()

    def forward(j):
        for i in range(1, 4):
            slot_wait(core, (x + i) % 4, j)
            fwd_copy(i, j).start()

    def take(j):
        for i in range(4):
            slot_wait(1 - core, (x + i) % 4, j)

    @pl.when(late)
    def _():
        for j in range(CHUNKS):
            swap_copy(j).start()

    @pl.when(early)
    def _():
        for j in range(CHUNKS):
            send_own(j)

    wp_load.start()
    wo_load.start()

    owner = cuser_ref[...]
    is_user = owner == iota((32, CAND), 0)
    users = onehot(is_user)
    before = dot(users, onehot(iota((CAND, CAND), 0) < iota((CAND, CAND), 1)))
    within = jnp.sum(jnp.where(is_user, before, 0.0), axis=0, keepdims=True).astype(I32)
    smaller = dot(onehot(iota((32, 32), 1) < iota((32, 32), 0)), users)
    start = jnp.sum(smaller, axis=1, keepdims=True)
    place = jnp.sum(jnp.where(is_user, start, 0.0), axis=0, keepdims=True).astype(I32) + within
    part = place & 7
    code = owner * 32 + part * 4 + (within >> 3)
    sorted_at = ((part >> 1) << 7) + ((part & 1) << 6) + (place >> 3)

    def message(m):
        which, dy = m >> 2, m & 3
        pair = which >> 1
        dz = jnp.where(
            pair == 0, 0, jnp.where(pair == 1, 1, jnp.where(pair == 2, 7, jnp.where(which == 6, 2, 6)))
        )
        dcore = which & 1
        tz = (z + dz) & 7
        ty = (y + dy) & 3
        tcore = (core + dcore) & 1
        column = (tz & 3) * 4 + ty
        return column * 2 + (tz >> 2), tz >> 2, column * 2 + tcore, tcore

    slot = iota((CAND, 1), 0)
    to_user, _, _, to_core = message(slot >> 4)
    slot_code = to_user * 32 + (2 * x + to_core) * 4 + (slot & 3)
    match = slot_code == code
    slot_quarter = (slot >> 2) & 3
    cand_load.wait()
    sent = jnp.zeros((CAND, QUARTER), F32)
    for j in range(4):
        sent += dot(onehot(match & (slot_quarter == j)), candx[:, j * QUARTER : (j + 1) * QUARTER])
    msgs[...] = sent.astype(BF)

    def piece(ref, i):
        return ref.at[pl.ds(pl.multiple_of(i * 16, 16), 16)]

    def d_copy(m):
        _, tzh, tcand, _ = message(m)
        return remote(piece(msgs, m), piece(rdisp, c), d_send.at[0], d_recv.at[0], 2 * x + tzh, tcand)

    self_d = pltpu.make_async_copy(piece(msgs, 0), piece(rdisp, c), d_recv.at[0])
    self_d.start()

    def send_d(m, carry):
        d_copy(m).start()
        return carry

    lax.fori_loop(1, 32, send_d, 0)

    length = len_ref[user]

    def block_pos(kind, row):
        return (2 * ((row >> 5) & 3) + kind) * ROWS + (row >> 7) * CROWS + (row & (CROWS - 1))

    def project(kind, first, count):
        rows = pl.ds(pl.multiple_of((kind * 4 + first) * ROWS, ROWS), count * ROWS)
        alive = block_pos(kind, first * ROWS + iota((count * ROWS, 1), 0)) < length

        def step(n, carry):
            cols = pl.ds(pl.multiple_of(n * QUARTER, QUARTER), QUARTER)
            kcols = pl.ds(pl.multiple_of(3 * D + n * QUARTER, QUARTER), QUARTER)
            vcols = pl.ds(pl.multiple_of(D + n * QUARTER, QUARTER), QUARTER)
            keys[rows, cols] = silu(dot(xb[rows, :], wp[:, kcols])).astype(BF)
            values[rows, cols] = jnp.where(alive, silu(dot(xb[rows, :], wp[:, vcols])), 0.0).astype(BF)
            return carry

        lax.fori_loop(0, 4, step, 0, unroll=4)

    def project_q(rows_ref):
        def step(n, carry):
            cols = pl.ds(pl.multiple_of(n * QUARTER, QUARTER), QUARTER)
            qcols = pl.ds(pl.multiple_of(D + n * QUARTER, QUARTER), QUARTER)
            wcols = pl.ds(pl.multiple_of(2 * D + n * QUARTER, QUARTER), QUARTER)
            qg[:, qcols] = silu(dot(rows_ref[...], wp[:, wcols])).astype(BF)
            qg[:, cols] = silu(dot(rows_ref[...], wp[:, cols])).astype(BF)
            return carry

        lax.fori_loop(0, 4, step, 0, unroll=4)

    def attend(top, count, allowed, first):
        rows = pl.ds(top, count)
        for h in range(HEADS):
            cols = slice(h * HEAD, (h + 1) * HEAD)
            scores = lax.dot_general(
                qg[:, D + h * HEAD : D + (h + 1) * HEAD], keys[rows, cols], NT, preferred_element_type=F32
            )
            weights = silu(scores * HEAD ** -0.5)
            if allowed is not None:
                weights = jnp.where(allowed, weights, 0.0)
            mixed = dot(weights.astype(BF), values[rows, cols])
            if first:
                acc[:, cols] = mixed
            else:
                acc[:, cols] += mixed

    def pair_top(kind, pair):
        return pl.multiple_of((kind * 2 + pair) * 2 * ROWS, 2 * ROWS)

    wp_load.wait()
    for j in range(CHUNKS):
        @pl.when(late)
        def _():
            swap_copy(j).wait_recv()
            send_own(j)
            take(j)

        @pl.when(early)
        def _():
            forward(j)

        project(zh, j, 1)

    def late_forward(j):
        @pl.when(late)
        def _():
            forward(j)

    def early_take(j):
        @pl.when(early)
        def _():
            take(j)

    late_forward(0)

    pltpu.make_async_copy(rdisp, rdisp, d_recv.at[0]).wait()
    here = iota((ROWS, CAND), 0)
    lane = iota((ROWS, CAND), 1)
    same = ((here >> 2) == (lane >> 4)) & ((here & 3) == (lane & 3))
    lane_quarter = (lane >> 2) & 3
    for j in range(4):
        xc[:, j * QUARTER : (j + 1) * QUARTER] = dot(onehot(same & (lane_quarter == j)), rdisp[...]).astype(BF)
    project_q(xc)
    late_forward(1)
    attend(pair_top(zh, 0), 4 * ROWS, None, True)
    late_forward(2)
    late_forward(3)
    early_take(0)
    early_take(1)
    project(1 - zh, 0, 2)
    attend(pair_top(1 - zh, 0), 2 * ROWS, None, False)
    early_take(2)
    early_take(3)
    project(1 - zh, 2, 2)
    attend(pair_top(1 - zh, 1), 2 * ROWS, None, False)
    wo_load.wait()

    def normalise():
        totals = acc[...]
        average = jnp.mean(totals, axis=1, keepdims=True)
        centred = totals - average
        variance = jnp.mean(centred * centred, axis=1, keepdims=True)
        normed_ref[...] = (
            centred * lax.rsqrt(variance + 1e-05) * gain_ref[...] * qg[:, 0:D].astype(F32)
        ).astype(BF)

    def finish(rows_ref, cols):
        return (dot(normed_ref[...], wo[:, cols]) + rows_ref[:, cols].astype(F32)).astype(BF)

    normalise()
    tall = iota((CAND, ROWS), 0)
    wide = iota((CAND, ROWS), 1)
    same_t = ((wide >> 2) == (tall >> 4)) & ((wide & 3) == (tall & 3))
    tall_quarter = (tall >> 2) & 3
    my_ret = user * 2 + core

    def r_copy(i, part):
        there = (c + i) & 31
        return remote(
            piece(back, part * 32 + there), piece(rret, part * 64 + my_ret), r_send.at[part],
            r_recv.at[part], 2 * x + ((zh + (i >> 5)) & 1), there,
        )

    def self_r(part):
        return pltpu.make_async_copy(
            piece(back, part * 32 + c), piece(rret, part * 64 + my_ret), r_recv.at[part]
        )

    for part in range(PARTS):
        done = finish(xc, slice(part * WIDE, (part + 1) * WIDE))
        returned = jnp.zeros((CAND, PIECE), F32)
        for j in range(4):
            returned += dot(onehot(same_t & (tall_quarter == j)), done[:, j * PIECE : (j + 1) * PIECE])
        back[part * CAND : (part + 1) * CAND, :] = returned.astype(BF)
        self_r(part).start()

        def send_r(i, carry):
            r_copy(i, part).start()
            return carry

        lax.fori_loop(1, 64, send_r, 0, unroll=7)

    ret = iota((1024, 1), 0)
    ret_to = ret >> 4
    ret_code = (ret_to >> 1) * 32 + (2 * x + (ret_to & 1)) * 4 + (ret & 3)
    mine = iota((ROWS, 1), 0)
    mine_place = 8 * (mine & 63) + 2 * x + (mine >> 6)
    places = lax.dot_general(
        onehot(mine_place == place), onehot(ret_code == code), NT, preferred_element_type=F32
    )
    ret_quarter = (iota((ROWS, 1024), 1) >> 2) & 3
    for j in range(4):
        crep[j * ROWS : (j + 1) * ROWS, :] = jnp.where(ret_quarter == j, places, 0.0).astype(BF)
    order_ref[...] = sorted_at

    for j in range(CHUNKS):
        xh[j * CROWS : (j + 1) * CROWS, :] = slot_rows(core, x, j)[...]
    project_q(xh)
    query_pos = (2 * x + core) * ROWS + iota((ROWS, 1), 0)
    key = iota((1, 8 * ROWS), 1)
    attend(0, 8 * ROWS, block_pos(key >> 9, key & 511) <= query_pos, True)
    normalise()
    hist_tmp[...] = finish(xh, slice(0, D))
    hist_copy = remote(hist_tmp, hist_ref, h_sem.at[0], h_sem.at[1], swap_seq, user)

    hist_home = pltpu.make_async_copy(hist_tmp, hist_ref, h_sem.at[0])

    @pl.when(early)
    def _():
        hist_home.start()

    def sorted_part(part, there):
        return sorted_rows.at[pl.ds(pl.multiple_of(part * CAND + there * ROWS, ROWS), ROWS)]

    def picked_part(part):
        return picked_rows.at[part * ROWS : (part + 1) * ROWS]

    def g_home(part):
        return pltpu.make_async_copy(picked_part(part), sorted_part(part, x), g_send.at[part * 4])

    def g_copy(i, part):
        return remote(
            picked_part(part), sorted_part(part, x), g_send.at[part * 4 + i], g_recv.at[part * 4 + x], 2 * ((x + i) % 4) + zh, c
        )

    for part in range(PARTS):
        arrived = rret.at[part * 1024 : (part + 1) * 1024]
        pltpu.make_async_copy(arrived, arrived, r_recv.at[part]).wait()
        picked = dot(crep[...], rret[part * 1024 : (part + 1) * 1024, :]).astype(BF)
        for j in range(4):
            picked_rows[part * ROWS : (part + 1) * ROWS, j * PIECE : (j + 1) * PIECE] = picked[
                j * ROWS : (j + 1) * ROWS, :
            ]
        for i in range(1, 4):
            g_copy(i, part).start()
        g_home(part).start()

    @pl.when(late)
    def _():
        hist_copy.start()

    for part in range(PARTS):
        for i in range(1, 4):
            from_x = (x + i) % 4
            rows = sorted_part(part, from_x)
            remote(rows, rows, g_send.at[0], g_recv.at[part * 4 + from_x], s, other_core).wait_recv()

    for part in range(PARTS):
        for i in range(1, 4):
            g_copy(i, part).wait_send()
        g_home(part).wait()

        gone = rret.at[pl.ds(part * 1024, 63 * 16)]
        remote(gone, gone, r_send.at[part], r_recv.at[part], s, other_core).wait_send()

    left = rdisp.at[pl.ds(0, 31 * 16)]
    remote(left, left, d_send.at[0], d_recv.at[0], s, other_core).wait_send()
    for j in range(CHUNKS):
        for i in range(4):
            own_copy(i, j).wait_send()
        for i in range(1, 4):
            fwd_copy(i, j).wait_send()

    @pl.when(late)
    def _():
        for j in range(CHUNKS):
            swap_copy(j).wait_send()
        hist_copy.wait()

    @pl.when(early)
    def _():
        hist_home.wait()


def last_kernel(order_ref, rows_hbm, hist_hbm, hist_ref, cand_ref, rows, out, hist, load_sem, store_sem):
    hist_load = pltpu.make_async_copy(hist_hbm, hist, load_sem.at[4])
    hist_load.start()
    loads, stores = [], []
    for n in range(PARTS):
        src = rows_hbm.at[pl.ds(n * CAND, CAND)]
        loads.append(pltpu.make_async_copy(src, rows.at[n], load_sem.at[n]))
        loads[n].start()
    unsort = lax.dot_general(
        onehot(iota((CAND, CAND), 0) == iota((CAND, CAND), 1)),
        onehot(iota((CAND, 1), 0) == order_ref[...]), NT, preferred_element_type=F32,
    ).astype(BF)
    for n in range(PARTS):
        loads[n].wait()
        out[n] = dot(unsort, rows[n]).astype(BF)
        stores.append(
            pltpu.make_async_copy(out.at[n], cand_ref.at[:, pl.ds(n * WIDE, WIDE)], store_sem.at[n])
        )
        stores[-1].start()
        if n == 0:
            hist_load.wait()
            stores.append(pltpu.make_async_copy(hist, hist_ref, store_sem.at[4]))
            stores[1].start()
    for store in stores:
        store.wait()


def per_device(hist_x, hist_len, cand_x, cand_user, w_proj, w_out, norm_gain):
    any_spec = pl.BlockSpec(memory_space=pl.ANY)
    vmem = pl.BlockSpec(memory_space=pltpu.VMEM)
    dma = pltpu.SemaphoreType.DMA
    hist_rows, sorted_rows, order = pl.pallas_call(
        kernel,
        out_shape=(
            jax.ShapeDtypeStruct((ROWS, D), BF),
            jax.ShapeDtypeStruct((PARTS * CAND, WIDE), BF),
            jax.ShapeDtypeStruct((1, CAND), I32),
        ),
        in_specs=[any_spec, pl.BlockSpec(memory_space=pltpu.SMEM), any_spec, vmem, any_spec, any_spec, vmem],
        out_specs=(any_spec, any_spec, vmem),
        scratch_shapes=[
            pltpu.VMEM((D, 4 * D), BF),
            pltpu.VMEM((D, D), BF),
            pltpu.VMEM((CAND, D), BF),
            pltpu.VMEM((8 * ROWS, D), BF),
            pltpu.VMEM((8 * ROWS, D), BF),
            pltpu.VMEM((8 * ROWS, D), BF),
            pltpu.VMEM((ROWS, D), BF),
            pltpu.VMEM((ROWS, D), BF),
            pltpu.VMEM((ROWS, 2 * D), BF),
            pltpu.VMEM((ROWS, D), F32),
            pltpu.VMEM((ROWS, D), BF),
            pltpu.VMEM((CAND, QUARTER), BF),
            pltpu.VMEM((CAND, QUARTER), BF),
            pltpu.VMEM((PARTS * CAND, PIECE), BF),
            pltpu.VMEM((2 * PARTS * CAND, PIECE), BF),
            pltpu.VMEM((4 * ROWS, 2 * CAND), BF),
            pltpu.VMEM((PARTS * ROWS, WIDE), BF),
            pltpu.VMEM((ROWS, D), BF),
            dma((3 + CHUNKS,)),
            dma((CHUNKS,)),
            dma((CHUNKS,)),
            dma((4 * CHUNKS,)),
            dma((8 * CHUNKS,)),
            dma((3 * CHUNKS,)),
            dma((1,)),
            dma((1,)),
            dma((PARTS,)),
            dma((PARTS,)),
            dma((PARTS * 4,)),
            dma((PARTS * 4,)),
            dma((2,)),
        ],
        compiler_params=pltpu.CompilerParams(
            collective_id=0, has_side_effects=True, vmem_limit_bytes=56 * 2**20
        ),
    )(
        hist_x.reshape(ROWS, D), hist_len, cand_x, cand_user.reshape(1, CAND), w_proj, w_out,
        norm_gain.reshape(1, D),
    )
    hist_out, cand_out = pl.pallas_call(
        last_kernel,
        out_shape=(jax.ShapeDtypeStruct((ROWS, D), BF), jax.ShapeDtypeStruct((CAND, D), BF)),
        in_specs=[vmem, any_spec, any_spec],
        out_specs=(any_spec, any_spec),
        scratch_shapes=[
            pltpu.VMEM((PARTS, CAND, WIDE), BF),
            pltpu.VMEM((PARTS, CAND, WIDE), BF),
            pltpu.VMEM((ROWS, D), BF),
            dma((5,)),
            dma((5,)),
        ],
        compiler_params=pltpu.CompilerParams(vmem_limit_bytes=56 * 2**20),
    )(order, sorted_rows, hist_rows)
    return hist_out[None], cand_out


def solution(mesh):
    in_specs = (P("cand", "seq", None), P(), P("cand", None), P("cand", None), P(), P(), P())
    out_specs = (P("cand", "seq", None), P("cand", None))
    return jax.shard_map(
        per_device, mesh=mesh, in_specs=in_specs, out_specs=out_specs, check_vma=False
    )
```
